128 devices in a mesh: pp: 16 (over y_hi, z, core), tp: 8 (over y_lo, x).
Axes of the slice: x: 4, y: 4 (y_hi: 2, y_lo: 2; y = y_hi * 2 + y_lo), z: 4, core: 2. Of those that a mesh axis runs over, the one named last changes fastest.
Arguments:
- queries: bfloat16 [16, 3, 512, 8192], P('pp', None, None, 'tp')
- attention_output_grads: bfloat16 [16, 3, 512, 8192], P('pp', None, None, 'tp'), may hold values from -6 to 6
- keys: bfloat16 [16, 3, 512, 1024], P('pp', None, None, 'tp')
- hidden: bfloat16 [16, 3, 512, 8192], P('pp', None, None, 'tp'), may hold values from -6 to 6
- value_weight: bfloat16 [16, 3, 8192, 1024], P('pp', None, 'tp'), may hold values from -0.1875 to 0.1875
- value_down_matrix: bfloat16 [16, 3, 8192, 64], P('pp', None, 'tp'), may hold values from -0.0625 to 0.0625
- value_up_matrix: bfloat16 [16, 3, 64, 1024], P('pp'), may hold values from -0.75 to 0.75
- document_index: int32 [512], replicated, may hold values from 0 to 7, never falling along the last dimension, each value on 1 to 256 neighbouring positions
- advantage: int32 [512], replicated, may hold values from -3 to 3
- loss_token_mask: int32 [512], replicated, may hold values 0 or 1
- top_stream_gradient: bfloat16 [512, 8192], P(None, 'tp'), may hold values from -6 to 6
Outputs:
- grad_in: bfloat16 [16, 3, 512, 8192], P('pp', None, None, 'tp')
- lora_a_grad: float32 [16, 3, 8192, 64], P('pp', None, 'tp')
- lora_b_grad: float32 [16, 3, 64, 1024], P('pp', None, None, 'tp')
The draws below stay inside these ranges and needn't reach their ends.
All inputs are finite; a program needn't handle non-finite values.
Results may differ from the reference program's by a relative error of at most 0.019.
Values may be sent and summed in bfloat16 or wider, within the bound.
A program may use at most 448 MiB of HBM per device.

```python
import math
import jax
import jax.numpy as jnp
import numpy as np
from jax import lax

MODEL_DIM = 8192
HD = 128
KVH = 8
QPK = 8
ADAPTER_RANK = 64
SECTION_LAYERS = 3
SEGS = 8
TOKENS_MB = 512
VALUE_COLUMNS = 1024
QCOLS = 8192
N_PP = 16


def shared_keys(key):
    return jax.random.normal(key, (N_PP, SECTION_LAYERS, TOKENS_MB, KVH * HD), jnp.float32)


def draw_keys(key, part):
    base_keys = shared_keys(key)
    return base_keys.astype(jnp.bfloat16)


def draw_queries(key, part):
    key = jax.random.fold_in(key, 23)
    fresh = jax.random.normal(key, (N_PP, SECTION_LAYERS, TOKENS_MB, KVH * QPK * HD), jnp.float32)
    return fresh.astype(jnp.bfloat16)


def set_ends(entries, stream_key, smallest, high):
    extent = entries.shape
    place = [jax.random.randint(jax.random.fold_in(stream_key, axis), (), 0, extent[axis]) for axis in range(len(extent))]
    entries = entries.at[tuple(place)].set(smallest)
    longest = extent.index(max(extent))
    place[longest] = (place[longest] + 1) % extent[longest]
    return entries.at[tuple(place)].set(high)


def shard_levels(own_key, dims, split, smallest, top_value):
    factor_of, own = 1.0, jax.random.fold_in(own_key, 6)
    for dim, blocks in split:
        draws = jnp.exp(jax.random.uniform(jax.random.fold_in(own, dim), (blocks,), jnp.float32, smallest / len(split), top_value / len(split)))
        factor_of = factor_of * jnp.repeat(draws, dims[dim] // blocks).reshape([-1 if axis == dim else 1 for axis in range(len(dims))])
    return factor_of


def length_profile(number_of, total, most, slope):
    weights = [(1 << 20) // math.isqrt(rank ** slope) + 1 for rank in range(2, number_of + 1)]
    rest, given = total - most - (number_of - 1), [1] * (number_of - 1)
    while rest > 0:
        movable = [i for i in range(number_of - 1) if given[i] < most]
        whole, left = sum([weights[i] for i in movable]), rest
        for i in movable:
            extra = min(most - given[i], max(1, left * weights[i] // whole), rest)
            given[i] = given[i] + extra
            rest = rest - extra
    return np.array([most] + given)


def uneven(key, number_of, total, limit, lean):
    if number_of == 2:
        one = jax.random.randint(key, (), max(1, total - limit), min(limit, total - 1) + 1)
        return jnp.stack([one, total - one])
    lengths = jnp.asarray(length_profile(number_of, total, limit, lean), jnp.int32)
    twos = (number_of - 1) // 2
    donor, sink = lengths[1:1 + 2 * twos:2], lengths[2:2 + 2 * twos:2]
    room = jnp.minimum(donor - 1, limit - sink)
    shifted = jax.random.randint(jax.random.fold_in(key, 1), (twos,), 0, 1 << 20) % (room + 1)
    lengths = lengths.at[1:1 + 2 * twos:2].set(donor - shifted).at[2:2 + 2 * twos:2].set(sink + shifted)
    return lengths[jax.random.permutation(jax.random.fold_in(key, 2), number_of)]


def noise(stream_key, shape, width, most, split=(), kind=jnp.bfloat16):
    loudness = shard_levels(stream_key, shape, split, -0.22, 0.18) if split else 1.0
    drawn = jax.random.normal(stream_key, shape, jnp.float32) * width * loudness
    return jnp.minimum(jnp.maximum(drawn, -most), most).astype(kind)


def setup_inputs(seed: int = 0) -> dict:
    seeds = jax.random.split(jax.random.key(seed), 12)
    queries = draw_queries(jax.random.fold_in(seeds[11], 71), 0)
    attention_output_grads = noise(seeds[1], (N_PP, SECTION_LAYERS, TOKENS_MB, QCOLS), 1.0, 6.0, ((0, 16), (3, 8)))
    keys = draw_keys(jax.random.fold_in(seeds[11], 71), 0)
    hidden = noise(seeds[3], (N_PP, SECTION_LAYERS, TOKENS_MB, MODEL_DIM), 1.0, 6.0, ((0, 16), (3, 8)))
    value_weight = noise(seeds[4], (N_PP, SECTION_LAYERS, MODEL_DIM, VALUE_COLUMNS), VALUE_COLUMNS ** -0.5, 0.1875, ((0, 16), (2, 8)))
    value_down_matrix = noise(seeds[5], (N_PP, SECTION_LAYERS, MODEL_DIM, ADAPTER_RANK), MODEL_DIM ** -0.5, 0.0625, ((0, 16), (2, 8)))
    value_up_matrix = noise(seeds[6], (N_PP, SECTION_LAYERS, ADAPTER_RANK, VALUE_COLUMNS), ADAPTER_RANK ** -0.5, 0.75, ((0, 16),))
    document_index = jnp.searchsorted(jnp.cumsum(uneven(seeds[7], SEGS, TOKENS_MB, TOKENS_MB // 2, 0)), jnp.arange(TOKENS_MB), side="right").astype(jnp.int32)
    advantage = set_ends(jax.random.randint(seeds[8], (TOKENS_MB,), -3, 4), jax.random.fold_in(seeds[8], 1), -3, 3).astype(jnp.int32)
    loss_token_mask = set_ends((jax.random.randint(seeds[9], (TOKENS_MB,), 0, 4) < 3).astype(jnp.int32), jax.random.fold_in(seeds[9], 1), 0, 1)
    top_stream_gradient = noise(seeds[10], (TOKENS_MB, MODEL_DIM), 1.0, 6.0, ((1, 8),))
    return {"queries": queries, "attention_output_grads": attention_output_grads, "keys": keys, "hidden": hidden, "value_weight": value_weight, "value_down_matrix": value_down_matrix, "value_up_matrix": value_up_matrix, "document_index": document_index, "advantage": advantage, "loss_token_mask": loss_token_mask, "top_stream_gradient": top_stream_gradient}


adapter_scale = 2.0
epsilon = 1e-05

def value_gradient(queries, keys, grads, document_index):
    total = keys.shape[0]
    groups = keys.shape[1] // HD
    block = min(512, total)
    key_heads = keys.reshape(total, groups, HD).astype(jnp.float32)
    positions = jnp.arange(total, dtype=jnp.int32)

    def one_block(carry, block_id):
        start = (block_id * block).astype(jnp.int32)
        query_block = lax.dynamic_slice_in_dim(queries, start, block, 0).reshape(block, groups, QPK, HD).astype(jnp.float32)
        grad_block = lax.dynamic_slice_in_dim(grads, start, block, 0).reshape(block, groups, QPK, HD).astype(jnp.float32)
        scores = jnp.einsum('bgqh,kgh->gqbk', query_block, key_heads) * HD ** (-0.5)
        row_pos = start + jnp.arange(block, dtype=jnp.int32)
        row_segs = lax.dynamic_slice_in_dim(document_index, start, block, 0)
        allowed = (positions[None, :] <= row_pos[:, None]) & (document_index[None, :] == row_segs[:, None])
        scores = jnp.where(allowed, scores, -1e+30)
        peak = lax.optimization_barrier(jnp.max(scores, axis=-1, keepdims=True))
        expo = jnp.exp(scores - peak)
        weights = (expo / lax.optimization_barrier(jnp.sum(expo, axis=-1, keepdims=True))).astype(jnp.bfloat16).astype(jnp.float32)
        return (carry + jnp.einsum('gqbk,bgqh->kgh', weights, grad_block), None)
    start_value = jnp.zeros((total, groups, HD), jnp.float32)
    result, unused = lax.scan(one_block, start_value, jnp.arange(total // block, dtype=jnp.int32))
    return result.reshape(total, groups * HD)

def reference(queries, attention_output_grads, keys, hidden, value_weight, value_down_matrix, value_up_matrix, document_index, advantage, loss_token_mask, top_stream_gradient):
    labels = jnp.arange(SEGS, dtype=jnp.int32)
    member = (document_index[:, None] == labels[None, :]).astype(jnp.float32)
    masked = loss_token_mask.astype(jnp.float32)
    counts = lax.optimization_barrier(jnp.sum(member * masked[:, None], axis=0))
    per_token = lax.optimization_barrier(jnp.sum(member * (1.0 / jnp.maximum(counts, 1.0))[None, :], axis=1))
    token_weight = advantage.astype(jnp.float32) * masked * per_token * (TOKENS_MB / SEGS)
    top_grad = token_weight[:, None] * top_stream_gradient.astype(jnp.float32)
    layer_count = N_PP * SECTION_LAYERS

    def flatten_layers(array):
        return array.reshape((layer_count,) + array.shape[2:])

    def single_layer(pieces):
        query_rows, grad_rows, key_rows, hidden_rows, weight_v, adapter_down, adapter_up = pieces
        stream = hidden_rows.astype(jnp.float32)
        inverse_rms = lax.rsqrt(lax.optimization_barrier(jnp.mean(stream * stream, axis=1)) + epsilon)
        normed = stream * inverse_rms[:, None]
        normalized_up = normed.astype(jnp.bfloat16)
        value_stream_gradient = value_gradient(query_rows, key_rows, grad_rows, document_index).astype(jnp.bfloat16)
        adapter_upward = jnp.dot(value_stream_gradient, adapter_up.T, preferred_element_type=jnp.float32).astype(jnp.bfloat16)
        normalized_gradient = jnp.dot(value_stream_gradient, weight_v.T, preferred_element_type=jnp.float32)
        normalized_gradient = normalized_gradient + adapter_scale * jnp.dot(adapter_upward, adapter_down.T, preferred_element_type=jnp.float32)
        inner = lax.optimization_barrier(jnp.mean(normed * normalized_gradient, axis=1, keepdims=True))
        term = (inverse_rms[:, None] * (normalized_gradient - normed * inner)).astype(jnp.bfloat16)
        down_gradient = adapter_scale * jnp.dot(normalized_up.T, adapter_upward, preferred_element_type=jnp.float32)
        reduced_up = jnp.dot(normalized_up, adapter_down, preferred_element_type=jnp.float32).astype(jnp.bfloat16)
        up_gradient = adapter_scale * jnp.dot(reduced_up.T, value_stream_gradient, preferred_element_type=jnp.float32)
        return (term, down_gradient, up_gradient)
    gradient_terms, down_gradients, up_gradients = lax.map(single_layer, (flatten_layers(queries), flatten_layers(attention_output_grads), flatten_layers(keys), flatten_layers(hidden), flatten_layers(value_weight), flatten_layers(value_down_matrix), flatten_layers(value_up_matrix)))
    ordered = jnp.swapaxes(gradient_terms.reshape(N_PP, SECTION_LAYERS, TOKENS_MB, MODEL_DIM), 0, 1).reshape(layer_count, TOKENS_MB, MODEL_DIM)

    def descend(carry, term):
        carry = carry + term.astype(jnp.float32)
        return (carry, carry.astype(jnp.bfloat16))
    unused, grads = lax.scan(descend, top_grad, ordered, reverse=True)
    grad_in = jnp.swapaxes(grads.reshape(SECTION_LAYERS, N_PP, TOKENS_MB, MODEL_DIM), 0, 1)
    return (grad_in, down_gradients.reshape(N_PP, SECTION_LAYERS, MODEL_DIM, ADAPTER_RANK), up_gradients.reshape(N_PP, SECTION_LAYERS, ADAPTER_RANK, KVH * HD))
```

```python
import jax
import jax.numpy as jnp
from jax import lax
from jax.experimental import pallas as pl
from jax.experimental.pallas import tpu as pltpu
from jax.sharding import PartitionSpec as P

MESH = pl.DeviceIdType.MESH
BF16 = jnp.bfloat16
F32 = jnp.float32
LAYERS = 3
TOKENS = 512
WIDTH = 1024
HEAD = 128
HEADS = 8
RANK = 64
HALF = 256
ROWS = 32
CHIPS = 8
TP = 8
MODEL = 8192
SEGS = 8
LOG2E = 1.4426950408889634
SOFTMAX_SCALE = HEAD**-0.5 * LOG2E
MASK_OFFSET = (0, 128, 384, 768)


def dot(a, b, dims):
    return lax.dot_general(a, b, (dims, ((), ())), preferred_element_type=F32)


def kernel(
    q_hbm, g_hbm, k_hbm, h_hbm, w_hbm, dn_hbm, up_hbm, top_hbm, doc_ref, adv_ref, loss_ref,
    out_hbm, la_hbm, lb_hbm,
    q_v, g_v, k_v, h_v, w_v, dn_v, up_v, top_v,
    mask_v, weight_v, acc_v, vg_v, hd_v, ad_v, ng_v, inv_v,
    sqs_v, sqr_v, ins_v, inr_v, lbs_v, lbr_v, la_v, lb_v,
    t_v, tp_v, p_v, q8_v, rs_v, rr_v, carry_v, own_v, peer_v,
    in_sem, out_sem,
    gs_sem, gr_sem, sqs_sem, sqr_sem, ins_sem, inr_sem, lbs_sem, lbr_sem,
    cs_sem, cr_sem, p1s_sem, p1r_sem, p2s_sem, p2r_sem, os_sem, or_sem,
):
    pp = lax.axis_index("pp")
    tp = lax.axis_index("tp")
    core = lax.rem(pp, 2)
    chip = lax.div(pp, 2)
    yl = lax.div(tp, 4)
    x = lax.rem(tp, 4)

    yl_peer = (pp, (1 - yl) * 4 + x)
    x_up = (pp, yl * 4 + lax.rem(x + 1, 4))
    x_down = (pp, yl * 4 + lax.rem(x + 3, 4))
    core_peer = (chip * 2 + (1 - core), tp)

    def tp_peer(j):
        return (pp, lax.rem(tp + j, TP))

    def chip_index(j):
        return lax.rem(chip + j, CHIPS)

    def chip_peer(j):
        return (chip_index(j) * 2 + core, tp)

    copies = {}

    def load(name, index, src, dst):
        copies[name] = pltpu.make_async_copy(src, dst, in_sem.at[index])
        copies[name].start()

    count = 0
    for l in (2, 1, 0):
        for name, src, dst in (("k", k_hbm, k_v), ("q", q_hbm, q_v), ("g", g_hbm, g_v)):
            load((name, l), count, src.at[l], dst.at[l])
            count += 1
        if l == 2:
            load("h", count, h_hbm, h_v)
            load("dn", count + 1, dn_hbm, dn_v)
            load("up", count + 2, up_hbm, up_v)
            count += 3
    for l in (2, 1, 0):
        load(("w", l), count, w_hbm.at[l], w_v.at[l])
        count += 1
    own_row = core * HALF + chip * ROWS
    load("top", count, top_hbm.at[pl.ds(pl.multiple_of(own_row, ROWS), ROWS)], top_v)

    barrier = pltpu.get_barrier_semaphore()
    for j in range(1, TP):
        pl.semaphore_signal(barrier, inc=1, device_id=tp_peer(j), device_id_type=MESH)
    for j in range(1, CHIPS):
        pl.semaphore_signal(barrier, inc=1, device_id=chip_peer(j), device_id_type=MESH)
    pl.semaphore_signal(barrier, inc=1, device_id=core_peer, device_id_type=MESH)

    def remote(src, dst, send, recv, device):
        return pltpu.make_async_remote_copy(
            src_ref=src, dst_ref=dst, send_sem=send, recv_sem=recv, device_id=device, device_id_type=MESH
        )

    def columns(row):
        return jnp.transpose(jnp.broadcast_to(row, (128, TOKENS)))

    def rows_of(sums):
        return jnp.sum(jnp.transpose(sums), axis=0, keepdims=True)

    doc_row = doc_ref[...].astype(F32)
    doc_col = columns(doc_row)
    key_pos = lax.broadcasted_iota(jnp.int32, (128, 128), 0)
    query_pos = lax.broadcasted_iota(jnp.int32, (128, 128), 1)
    for b in range(4):
        low = max(0, b - 2)
        for kb in range(low, b + 1):
            allowed = doc_col[128 * kb : 128 * kb + 128, :] == doc_row[:, 128 * b : 128 * b + 128]
            if kb == b:
                allowed = allowed & (key_pos <= query_pos)
            at = MASK_OFFSET[b] + 128 * (kb - low)
            mask_v[at : at + 128, :] = jnp.where(allowed, 0.0, -jnp.inf)
    loss_row = loss_ref[...].astype(F32)
    labels = lax.broadcasted_iota(jnp.int32, (SEGS, TOKENS), 0).astype(F32)
    member = jnp.where(labels == doc_row, 1.0, 0.0)
    counts = jnp.sum(member * loss_row, axis=1, keepdims=True)
    per_token = jnp.sum(member * (1.0 / jnp.maximum(counts, 1.0)), axis=0, keepdims=True)
    weight_v[...] = columns(adv_ref[...].astype(F32) * loss_row * per_token * (TOKENS / SEGS))

    slot = x * 2 + yl
    other = x * 2 + (1 - yl)
    left = lax.rem(x + 3, 4) * 2
    right = lax.rem(x + 1, 4) * 2
    across = lax.rem(x + 2, 4) * 2

    def attention(l):
        for name in ("k", "q", "g"):
            copies[(name, l)].wait()
        for b in range(4):
            low, high = max(0, b - 2) * 128, (b + 1) * 128
            keys = k_v[l, low:high, :]
            mask = mask_v[MASK_OFFSET[b] : MASK_OFFSET[b] + high - low, :]
            mask4 = jnp.concatenate([mask] * 4, axis=1)
            total = None
            for part in range(2):
                heads = range(4 * part, 4 * part + 4)
                block = slice(128 * b, 128 * b + 128)
                queries = jnp.concatenate([q_v[l, block, HEAD * i : HEAD * i + HEAD] for i in heads], axis=0)
                grads = jnp.concatenate([g_v[l, block, HEAD * i : HEAD * i + HEAD] for i in heads], axis=0)
                scores = dot(keys, queries, ((1,), (1,))) + mask4
                peak = jnp.max(scores, axis=0, keepdims=True)
                expo = jnp.exp2((scores - peak) * SOFTMAX_SCALE)
                probs = (expo * (1.0 / jnp.sum(expo, axis=0, keepdims=True))).astype(BF16)
                piece = dot(probs, grads, ((1,), (0,)))
                total = piece if total is None else total + piece
            if b == 0:
                acc_v[0:128, :] = total
            else:
                acc_v[low : high - 128, :] += total[: high - low - 128]
                acc_v[high - 128 : high, :] = total[high - low - 128 :]
        vg_v[l, slot] = acc_v[...].astype(BF16)

    def gather_copy(l, i, place, device):
        return remote(vg_v.at[l, place], vg_v.at[l, place], gs_sem.at[l, i], gr_sem.at[l, i], device)

    def gather_out(l, i):
        return (
            lambda: gather_copy(l, 0, slot, yl_peer),
            lambda: gather_copy(l, 1, slot, x_up),
            lambda: gather_copy(l, 2, slot, x_down),
            lambda: gather_copy(l, 3, other, x_up),
            lambda: gather_copy(l, 4, other, x_down),
            lambda: gather_copy(l, 5, left + yl, x_up),
            lambda: gather_copy(l, 6, right + (1 - yl), x_down),
        )[i]()

    def gather_in(l, i):
        place = (other, left + yl, right + yl, left + (1 - yl), right + (1 - yl), across + yl, across + (1 - yl))[i]
        return gather_copy(l, i, place, yl_peer)

    def gather_1(l):
        for i in (0, 1, 2):
            gather_out(l, i).start()

    def gather_2(l):
        gather_in(l, 0).wait_recv()
        for i in (3, 4):
            gather_out(l, i).start()

    def gather_3(l):
        gather_in(l, 1).wait_recv()
        gather_out(l, 5).start()
        gather_in(l, 4).wait_recv()
        gather_out(l, 6).start()

    def gather_end(l):
        for i in (2, 3, 5, 6):
            gather_in(l, i).wait_recv()

    def squares_and_low():
        sqs_v[...] = jnp.zeros((8, TOKENS), F32)
        copies["h"].wait()
        copies["dn"].wait()
        for l in range(LAYERS):
            sums = None
            for n in range(WIDTH // 128):
                part = h_v[l, :, 128 * n : 128 * n + 128].astype(F32)
                sums = part * part if sums is None else sums + part * part
            sqs_v[l : l + 1, :] = rows_of(sums)
            hd_v[l] = dot(h_v[l], dn_v[l], ((1,), (0,)))
        sqr_v[tp] = sqs_v[...]

    def squares_copy(j, place):
        return remote(sqs_v, sqr_v.at[place], sqs_sem.at[j - 1], sqr_sem.at[j - 1], tp_peer(j))

    def squares_send():
        for j in range(1, TP):
            squares_copy(j, tp).start()

    def squares_wait():
        for j in range(1, TP):
            squares_copy(j, lax.rem(tp - j + TP, TP)).wait_recv()
        total = sqr_v[0]
        for i in range(1, TP):
            total = total + sqr_v[i]
        inverse = lax.rsqrt(total * (1.0 / MODEL) + 1e-5)
        for l in range(LAYERS):
            inv_v[l] = columns(inverse[l : l + 1, :])

    def gathered(l):
        return jnp.concatenate([vg_v[l, (j % 4) * 2 + j // 4] for j in range(TP)], axis=1)

    def inner_copy(l, j, place):
        return remote(ins_v.at[l], inr_v.at[l, place], ins_sem.at[l, j - 1], inr_sem.at[l, j - 1], tp_peer(j))

    def products(l):
        if l == 2:
            copies["up"].wait()
        copies[("w", l)].wait()
        ad_v[l] = dot(gathered(l), up_v[l], ((1,), (1,))).astype(BF16)
        acc_v[...] = jnp.zeros((TOKENS, 128), F32)

        def one(n, unused):
            start = pl.multiple_of(n * 256, 256)
            rows = pl.ds(start, 256)
            twice = (ad_v[l].astype(F32) * 2.0).astype(BF16)
            ng = dot(gathered(l), w_v[l, rows, :], ((1,), (1,))) + dot(twice, dn_v[l, rows, :], ((1,), (1,)))
            ng_v[:, rows] = ng
            prod = h_v[l, :, rows].astype(F32) * ng
            acc_v[...] += prod[:, :128] + prod[:, 128:]
            return unused

        lax.fori_loop(0, WIDTH // 256, one, 0)
        ins_v[l] = jnp.broadcast_to(rows_of(acc_v[...]), (8, TOKENS))
        inr_v[l, tp] = ins_v[l]
        for j in range(1, TP):
            inner_copy(l, j, tp).start()

    def terms(l):
        for j in range(1, TP):
            inner_copy(l, j, lax.rem(tp - j + TP, TP)).wait_recv()
        total = inr_v[l, 0]
        for i in range(1, TP):
            total = total + inr_v[l, i]
        inv = inv_v[l]
        acc_v[...] = inv * inv * inv * columns(total[0:1, :]) * (1.0 / MODEL)

        def one(n, unused):
            cols = pl.ds(pl.multiple_of(n * 128, 128), 128)
            t_v[l, :, cols] = (inv_v[l] * ng_v[:, cols] - acc_v[...] * h_v[l, :, cols].astype(F32)).astype(BF16)
            return unused

        lax.fori_loop(0, WIDTH // 128, one, 0)

    def lora_b_copy(l, j, block, place):
        return remote(lbs_v.at[l, block], lbr_v.at[l, place], lbs_sem.at[l, j - 1], lbr_sem.at[l, j - 1], tp_peer(j))

    def adapters(l):
        inv = inv_v[l][:, :RANK]
        scaled = (2.0 * inv * ad_v[l].astype(F32)).astype(BF16)
        la_v[l] = jnp.transpose(dot(scaled, h_v[l], ((0,), (0,))))
        low = (2.0 * inv * hd_v[l]).astype(BF16)
        part = dot(low, gathered(l), ((0,), (0,)))
        for j in range(TP):
            lbs_v[l, j] = part[:, 128 * j : 128 * j + 128].astype(BF16)
        lbr_v[l, tp] = lbs_v[l, tp]
        for j in range(1, TP):
            lora_b_copy(l, j, lax.rem(tp + j, TP), tp).start()
        pltpu.make_async_copy(la_v.at[l], la_hbm.at[l], out_sem.at[l]).start()

    def adapters_end(l):
        for j in range(1, TP):
            lora_b_copy(l, j, 0, lax.rem(tp - j + TP, TP)).wait_recv()
        total = lbr_v[l, 0].astype(F32)
        for i in range(1, TP):
            total = total + lbr_v[l, i].astype(F32)
        lb_v[l] = total
        pltpu.make_async_copy(lb_v.at[l], lb_hbm.at[l], out_sem.at[LAYERS + l]).start()

    mine = pl.ds(pl.multiple_of(core * HALF, HALF), HALF)
    theirs = pl.ds(pl.multiple_of((1 - core) * HALF, HALF), HALF)

    def core_copy(l):
        return remote(t_v.at[l, theirs], tp_v.at[l], cs_sem.at[l], cr_sem.at[l], core_peer)

    def block(i):
        return pl.ds(pl.multiple_of(i * ROWS, ROWS), ROWS)

    def to_owner(l, j, place):
        return remote(p_v.at[l, block(chip_index(j))], q8_v.at[l, place], p1s_sem.at[l, j - 1], p1r_sem.at[l, j - 1], chip_peer(j))

    def from_owner(l, j, place):
        return remote(rs_v.at[l, chip_index(j)], rr_v.at[l, block(place)], p2s_sem.at[l, j - 1], p2r_sem.at[l, j - 1], chip_peer(j))

    def source(j):
        return lax.rem(chip - j + CHIPS, CHIPS)

    def pair_sums(l):
        core_copy(l).wait_recv()
        p_v[l] = (t_v[l, mine, :].astype(F32) + tp_v[l].astype(F32)).astype(BF16)
        for j in (4, 2, 6, 1, 3, 5, 7):
            to_owner(l, j, chip).start()
        q8_v[l, chip] = p_v[l, block(chip), :]

    def suffix(l):
        if l == LAYERS - 1:
            copies["top"].wait()
            weight = weight_v[pl.ds(pl.multiple_of(own_row, ROWS), ROWS), :]
            weights = jnp.concatenate([weight] * (WIDTH // 128), axis=1)
            carry = weights * top_v[...].astype(F32)
        else:
            carry = carry_v[...]
        for j in range(1, CHIPS):
            to_owner(l, j, source(j)).wait_recv()
        for i in reversed(range(CHIPS)):
            rs_v[l, i] = carry.astype(BF16)
            carry = carry + q8_v[l, i].astype(F32)
        carry_v[...] = carry
        for j in (4, 2, 6, 1, 3, 5, 7):
            from_owner(l, j, chip).start()
        rr_v[l, block(chip), :] = rs_v[l, chip]

    def out_copy(l):
        return remote(peer_v.at[l], out_hbm.at[l, mine], os_sem.at[l], or_sem.at[l], core_peer)

    def out_here(l):
        return pltpu.make_async_copy(own_v.at[l], out_hbm.at[l, mine], out_sem.at[2 * LAYERS + l])

    def finish(l):
        for j in range(1, CHIPS):
            from_owner(l, j, source(j)).wait_recv()
        first = (1 - core).astype(F32)
        second = core.astype(F32)
        carry = rr_v[l].astype(F32)
        term = t_v[l, mine, :].astype(F32)
        peer_term = tp_v[l].astype(F32)
        peer_v[l] = (carry + peer_term + second * term).astype(BF16)
        out_copy(l).start()
        own_v[l] = (carry + term + first * peer_term).astype(BF16)
        out_here(l).start()

    attention(2)
    pl.semaphore_wait(barrier, TP + CHIPS - 1)
    gather_1(2)
    squares_and_low()
    squares_send()
    gather_2(2)
    attention(1)
    gather_3(2)
    gather_1(1)
    attention(0)
    gather_2(1)
    squares_wait()
    gather_end(2)
    products(2)
    gather_3(1)
    gather_1(0)
    adapters(2)
    terms(2)
    core_copy(2).start()
    gather_2(0)
    gather_end(1)
    products(1)
    pair_sums(2)
    gather_3(0)
    adapters(1)
    terms(1)
    core_copy(1).start()
    gather_end(0)
    products(0)
    pair_sums(1)
    suffix(2)
    adapters(0)
    terms(0)
    core_copy(0).start()
    suffix(1)
    pair_sums(0)
    finish(2)
    suffix(0)
    finish(1)
    for l in (2, 1, 0):
        adapters_end(l)
    finish(0)

    for l in range(LAYERS):
        out_copy(l).wait_recv()
        out_copy(l).wait_send()
        out_here(l).wait()
        pltpu.make_async_copy(la_v.at[l], la_hbm.at[l], out_sem.at[l]).wait()
        pltpu.make_async_copy(lb_v.at[l], lb_hbm.at[l], out_sem.at[LAYERS + l]).wait()
        core_copy(l).wait_send()
        for i in range(7):
            gather_out(l, i).wait_send()
        for j in range(1, TP):
            inner_copy(l, j, tp).wait_send()
            lora_b_copy(l, j, lax.rem(tp + j, TP), tp).wait_send()
        for j in range(1, CHIPS):
            to_owner(l, j, chip).wait_send()
            from_owner(l, j, chip).wait_send()
    for j in range(1, TP):
        squares_copy(j, tp).wait_send()


def per_device(
    queries, attention_output_grads, keys, hidden, value_weight, value_down_matrix, value_up_matrix,
    document_index, advantage, loss_token_mask, top_stream_gradient,
):
    hbm = pl.BlockSpec(memory_space=pl.ANY)
    vmem = pl.BlockSpec(memory_space=pltpu.VMEM)
    dma = pltpu.SemaphoreType.DMA
    scratch = [
        pltpu.VMEM((LAYERS, TOKENS, WIDTH), BF16),
        pltpu.VMEM((LAYERS, TOKENS, WIDTH), BF16),
        pltpu.VMEM((LAYERS, TOKENS, HEAD), BF16),
        pltpu.VMEM((LAYERS, TOKENS, WIDTH), BF16),
        pltpu.VMEM((LAYERS, WIDTH, WIDTH), BF16),
        pltpu.VMEM((LAYERS, WIDTH, RANK), BF16),
        pltpu.VMEM((LAYERS, RANK, WIDTH), BF16),
        pltpu.VMEM((ROWS, WIDTH), BF16),
        pltpu.VMEM((1152, 128), F32),
        pltpu.VMEM((TOKENS, 128), F32),
        pltpu.VMEM((TOKENS, 128), F32),
        pltpu.VMEM((LAYERS, TP, TOKENS, HEAD), BF16),
        pltpu.VMEM((LAYERS, TOKENS, RANK), F32),
        pltpu.VMEM((LAYERS, TOKENS, RANK), BF16),
        pltpu.VMEM((TOKENS, WIDTH), F32),
        pltpu.VMEM((LAYERS, TOKENS, 128), F32),
        pltpu.VMEM((8, TOKENS), F32),
        pltpu.VMEM((TP, 8, TOKENS), F32),
        pltpu.VMEM((LAYERS, 8, TOKENS), F32),
        pltpu.VMEM((LAYERS, TP, 8, TOKENS), F32),
        pltpu.VMEM((LAYERS, TP, RANK, HEAD), BF16),
        pltpu.VMEM((LAYERS, TP, RANK, HEAD), BF16),
        pltpu.VMEM((LAYERS, WIDTH, RANK), F32),
        pltpu.VMEM((LAYERS, RANK, HEAD), F32),
        pltpu.VMEM((LAYERS, TOKENS, WIDTH), BF16),
        pltpu.VMEM((LAYERS, HALF, WIDTH), BF16),
        pltpu.VMEM((LAYERS, HALF, WIDTH), BF16),
        pltpu.VMEM((LAYERS, CHIPS, ROWS, WIDTH), BF16),
        pltpu.VMEM((LAYERS, CHIPS, ROWS, WIDTH), BF16),
        pltpu.VMEM((LAYERS, HALF, WIDTH), BF16),
        pltpu.VMEM((ROWS, WIDTH), F32),
        pltpu.VMEM((LAYERS, HALF, WIDTH), BF16),
        pltpu.VMEM((LAYERS, HALF, WIDTH), BF16),
        dma((16,)), dma((3 * LAYERS,)),
        dma((LAYERS, 7)), dma((LAYERS, 7)), dma((7,)), dma((7,)), dma((LAYERS, 7)), dma((LAYERS, 7)),
        dma((LAYERS, 7)), dma((LAYERS, 7)),
        dma((LAYERS,)), dma((LAYERS,)), dma((LAYERS, 7)), dma((LAYERS, 7)), dma((LAYERS, 7)), dma((LAYERS, 7)),
        dma((LAYERS,)), dma((LAYERS,)),
    ]
    grad_in, lora_a, lora_b = pl.pallas_call(
        kernel,
        name="value_backward",
        out_shape=(
            jax.ShapeDtypeStruct((LAYERS, TOKENS, WIDTH), BF16),
            jax.ShapeDtypeStruct((LAYERS, WIDTH, RANK), F32),
            jax.ShapeDtypeStruct((LAYERS, RANK, HEAD), F32),
        ),
        in_specs=[hbm] * 8 + [vmem] * 3,
        out_specs=(hbm, hbm, hbm),
        scratch_shapes=scratch,
        compiler_params=pltpu.CompilerParams(
            collective_id=0, has_side_effects=True, vmem_limit_bytes=60 << 20
        ),
        cost_estimate=pl.CostEstimate(flops=8_000_000_000, bytes_accessed=22_000_000, transcendentals=4_000_000),
    )(
        queries[0], attention_output_grads[0], keys[0], hidden[0], value_weight[0], value_down_matrix[0],
        value_up_matrix[0], top_stream_gradient,
        document_index.reshape(1, TOKENS), advantage.reshape(1, TOKENS), loss_token_mask.reshape(1, TOKENS),
    )
    return grad_in[None], lora_a[None], lora_b[None]


def solution(mesh):
    in_specs = (
        P("pp", None, None, "tp"),
        P("pp", None, None, "tp"),
        P("pp", None, None, "tp"),
        P("pp", None, None, "tp"),
        P("pp", None, "tp", None),
        P("pp", None, "tp", None),
        P("pp", None, None, None),
        P(),
        P(),
        P(),
        P(None, "tp"),
    )
    out_specs = (P("pp", None, None, "tp"), P("pp", None, "tp", None), P("pp", None, None, "tp"))
    return jax.shard_map(
        per_device, mesh=mesh, in_specs=in_specs, out_specs=out_specs, check_vma=False
    )
```

```python
import jax
import jax.numpy as jnp
from jax import lax
from jax.experimental import pallas as pl
from jax.experimental.pallas import tpu as pltpu
from jax.sharding import PartitionSpec as P

MESH = pl.DeviceIdType.MESH
BF16 = jnp.bfloat16
F32 = jnp.float32
LAYERS = 3
TOKENS = 512
WIDTH = 1024
HEAD = 128
HEADS = 8
RANK = 64
SPAN = 256
HALF = 128
ROWS = 16
CHIPS = 8
TP = 8
MODEL = 8192
SEGS = 8
LOG2E = 1.4426950408889634
CHUNKS = ((1, 0, 2), (2, 0, 2), (0, 0, 2))
SOFTMAX_SCALE = HEAD**-0.5 * LOG2E
MASK_OFFSET = (0, 128, 384, 768)


def dot(a, b, dims):
    return lax.dot_general(a, b, (dims, ((), ())), preferred_element_type=F32)


def kernel(
    q_hbm, g_hbm, k_hbm, h_hbm, w_hbm, dn_hbm, up_hbm, top_hbm, doc_ref, adv_ref, loss_ref,
    out_hbm, la_hbm, lb_hbm,
    q_v, g_v, k_v, h_v, w_v, dn_v, up_v, top_v,
    mask_v, weight_v, acc_v, vg_v, hd_v, ad_v, ng_v, inv_v,
    sqs_v, sqr_v, ins_v, inr_v, lbs_v, lbr_v, la_v, lb_v,
    t_v, tp_v, p_v, q8_v, rs_v, rr_v, carry_v, own_v, peer_v,
    in_sem, out_sem,
    gs_sem, gr_sem, sqs_sem, sqr_sem, ins_sem, inr_sem, lbs_sem, lbr_sem,
    cs_sem, cr_sem, p1s_sem, p1r_sem, p2s_sem, p2r_sem, os_sem, or_sem,
):
    pp = lax.axis_index("pp")
    tp = lax.axis_index("tp")
    core = lax.rem(pp, 2)
    chip = lax.div(pp, 2)
    yl = lax.div(tp, 4)
    x = lax.rem(tp, 4)

    yl_peer = (pp, (1 - yl) * 4 + x)
    x_up = (pp, yl * 4 + lax.rem(x + 1, 4))
    x_down = (pp, yl * 4 + lax.rem(x + 3, 4))
    core_peer = (chip * 2 + (1 - core), tp)

    def tp_peer(j):
        return (pp, lax.rem(tp + j, TP))

    def chip_index(j):
        return lax.rem(chip + j, CHIPS)

    def chip_peer(j):
        return (chip_index(j) * 2 + core, tp)

    copies = {}

    def load(name, src, dst):
        copies[name] = pltpu.make_async_copy(src, dst, in_sem.at[len(copies)])

    for l in (2, 1, 0):
        load(("k", l), k_hbm.at[l], k_v.at[l])
        load(("q", l), q_hbm.at[l], q_v.at[l])
        load(("g", l), g_hbm.at[l], g_v.at[l])
    load("h", h_hbm, h_v)
    load("dn", dn_hbm, dn_v)
    load("up", up_hbm, up_v)
    for l in (2, 1, 0):
        load(("w", l), w_hbm.at[l], w_v.at[l])
    load("top", top_hbm.at[:, core, chip], top_v)
    first = [(name, LAYERS - 1) for name in "kqg"]
    for name in first:
        copies[name].start()

    barrier = pltpu.get_barrier_semaphore()
    for j in range(1, TP):
        pl.semaphore_signal(barrier, inc=1, device_id=tp_peer(j), device_id_type=MESH)
    for j in range(1, CHIPS):
        pl.semaphore_signal(barrier, inc=1, device_id=chip_peer(j), device_id_type=MESH)
    pl.semaphore_signal(barrier, inc=1, device_id=core_peer, device_id_type=MESH)

    def remote(src, dst, send, recv, device):
        return pltpu.make_async_remote_copy(
            src_ref=src, dst_ref=dst, send_sem=send, recv_sem=recv, device_id=device, device_id_type=MESH
        )

    def columns(row):
        return jnp.transpose(jnp.broadcast_to(row, (128, TOKENS)))

    def rows_of(sums):
        parts = [sums[128 * i : 128 * i + 128, :] for i in range(sums.shape[0] // 128)]
        return jnp.concatenate([jnp.sum(jnp.transpose(part), axis=0, keepdims=True) for part in parts], axis=0)

    def columns_of(rows):
        return jnp.concatenate(
            [jnp.transpose(jnp.broadcast_to(rows[i : i + 1, :], (128, 128))) for i in range(rows.shape[0])], axis=0
        )

    doc_row = doc_ref[...].astype(F32)
    doc_col = columns(doc_row)
    key_pos = lax.broadcasted_iota(jnp.int32, (128, 128), 0)
    query_pos = lax.broadcasted_iota(jnp.int32, (128, 128), 1)
    for b in range(4):
        low = max(0, b - 2)
        for kb in range(low, b + 1):
            allowed = doc_col[128 * kb : 128 * kb + 128, :] == doc_row[:, 128 * b : 128 * b + 128]
            if kb == b:
                allowed = allowed & (key_pos <= query_pos)
            at = MASK_OFFSET[b] + 128 * (kb - low)
            mask_v[at : at + 128, :] = jnp.where(allowed, 0.0, -jnp.inf)
    loss_row = loss_ref[...].astype(F32)
    labels = lax.broadcasted_iota(jnp.int32, (SEGS, TOKENS), 0).astype(F32)
    member = jnp.where(labels == doc_row, 1.0, 0.0)
    counts = jnp.sum(member * loss_row, axis=1, keepdims=True)
    per_token = jnp.sum(member * (1.0 / jnp.maximum(counts, 1.0)), axis=0, keepdims=True)
    weights = columns(adv_ref[...].astype(F32) * loss_row * per_token * (TOKENS / SEGS))
    weight_v[...] = weights.reshape(2, 2, CHIPS, ROWS, 128)

    slot = x * 2 + yl
    other = x * 2 + (1 - yl)
    left = lax.rem(x + 3, 4) * 2
    right = lax.rem(x + 1, 4) * 2
    across = lax.rem(x + 2, 4) * 2

    def attention(l):
        for name in ("k", "q", "g"):
            copies[(name, l)].wait()
        if l == LAYERS - 1:
            for name in copies:
                if name not in first:
                    copies[name].start()
        for b in range(4):
            low, high = max(0, b - 2) * 128, (b + 1) * 128
            keys = k_v[l, low:high, :]
            mask = mask_v[MASK_OFFSET[b] : MASK_OFFSET[b] + high - low, :]
            mask4 = jnp.concatenate([mask] * 4, axis=1)
            total = None
            for part in range(2):
                heads = range(4 * part, 4 * part + 4)
                block = slice(128 * b, 128 * b + 128)
                queries = jnp.concatenate([q_v[l, block, HEAD * i : HEAD * i + HEAD] for i in heads], axis=0)
                grads = jnp.concatenate([g_v[l, block, HEAD * i : HEAD * i + HEAD] for i in heads], axis=0)
                scores = dot(keys, queries, ((1,), (1,))) + mask4
                peak = jnp.max(scores, axis=0, keepdims=True)
                expo = jnp.exp2((scores - peak) * SOFTMAX_SCALE)
                probs = (expo * (1.0 / jnp.sum(expo, axis=0, keepdims=True))).astype(BF16)
                piece = dot(probs, grads, ((1,), (0,)))
                total = piece if total is None else total + piece
            if b == 0:
                acc_v[0:128, :] = total
            else:
                acc_v[low : high - 128, :] += total[: high - low - 128]
                acc_v[high - 128 : high, :] = total[high - low - 128 :]
        vg_v[l, slot] = acc_v[...].astype(BF16)

    def spans(chunk):
        return pl.ds(chunk[1], chunk[2])

    def tokens(chunk):
        return slice(chunk[1] * SPAN, (chunk[1] + chunk[2]) * SPAN)

    def index(chunk):
        return chunk[0] * 2 + chunk[1]

    def gather_copy(chunk, i, place, device):
        part = vg_v.at[chunk[0], place, pl.ds(chunk[1] * SPAN, chunk[2] * SPAN)]
        return remote(part, part, gs_sem.at[index(chunk), i], gr_sem.at[index(chunk), i], device)

    def gather_out(chunk, i):
        return (
            lambda: gather_copy(chunk, 0, slot, yl_peer),
            lambda: gather_copy(chunk, 1, slot, x_up),
            lambda: gather_copy(chunk, 2, slot, x_down),
            lambda: gather_copy(chunk, 3, other, x_up),
            lambda: gather_copy(chunk, 4, other, x_down),
            lambda: gather_copy(chunk, 5, left + yl, x_up),
            lambda: gather_copy(chunk, 6, right + (1 - yl), x_down),
        )[i]()

    def gather_in(chunk, i):
        place = (other, left + yl, right + yl, left + (1 - yl), right + (1 - yl), across + yl, across + (1 - yl))[i]
        return gather_copy(chunk, i, place, yl_peer)

    def gather_1(chunk):
        for i in (0, 1, 2):
            gather_out(chunk, i).start()

    def gather_2(chunk):
        gather_in(chunk, 0).wait_recv()
        for i in (3, 4):
            gather_out(chunk, i).start()

    def gather_3(chunk):
        gather_in(chunk, 1).wait_recv()
        gather_out(chunk, 5).start()

    def gather_4(chunk):
        gather_in(chunk, 4).wait_recv()
        gather_out(chunk, 6).start()

    def gather_end(chunk):
        for i in (2, 3, 5, 6):
            gather_in(chunk, i).wait_recv()

    def squares_and_low():
        sqs_v[...] = jnp.zeros((16, 128), F32)
        copies["h"].wait()
        copies["dn"].wait()
        for l in range(LAYERS):
            sums = None
            for n in range(WIDTH // 128):
                part = h_v[l, :, 128 * n : 128 * n + 128].astype(F32)
                sums = part * part if sums is None else sums + part * part
            sqs_v[4 * l : 4 * l + 4, :] = rows_of(sums)
            hd_v[l] = dot(h_v[l], dn_v[l], ((1,), (1,)))
        sqr_v[tp] = sqs_v[...]

    def squares_copy(j, place):
        return remote(sqs_v, sqr_v.at[place], sqs_sem.at[j - 1], sqr_sem.at[j - 1], tp_peer(j))

    def squares_send():
        for j in range(1, TP):
            squares_copy(j, tp).start()

    def squares_wait():
        for j in range(1, TP):
            squares_copy(j, lax.rem(tp - j + TP, TP)).wait_recv()
        total = sqr_v[0]
        for i in range(1, TP):
            total = total + sqr_v[i]
        inverse = lax.rsqrt(total * (1.0 / MODEL) + 1e-5)
        for l in range(LAYERS):
            inv_v[l] = columns_of(inverse[4 * l : 4 * l + 4, :])

    def gathered(l, rows):
        return jnp.concatenate([vg_v[l, (j % 4) * 2 + j // 4, rows] for j in range(TP)], axis=1)

    def inner_copy(chunk, j, place):
        at = index(chunk)
        return remote(ins_v.at[at], inr_v.at[at, place], ins_sem.at[at, j - 1], inr_sem.at[at, j - 1], tp_peer(j))

    def products(chunk):
        l, at, rows = chunk[0], index(chunk), tokens(chunk)
        if l == LAYERS - 1 and chunk[1] == 0:
            copies["up"].wait()
        if chunk[1] == 0:
            copies[("w", l)].wait()
        ad_v[l, rows] = dot(gathered(l, rows), up_v[l], ((1,), (1,))).astype(BF16)
        acc_v[rows] = jnp.zeros((chunk[2] * SPAN, 128), F32)

        def one(n, unused):
            cols = pl.ds(pl.multiple_of(n * 256, 256), 256)
            twice = (ad_v[l, rows].astype(F32) * 2.0).astype(BF16)
            ng = dot(gathered(l, rows), w_v[l, cols, :], ((1,), (1,))) + dot(twice, dn_v[l, :, cols], ((1,), (0,)))
            ng_v[l % 2, rows, cols] = ng
            prod = h_v[l, rows, cols].astype(F32) * ng
            acc_v[rows] += prod[:, :128] + prod[:, 128:]
            return unused

        lax.fori_loop(0, WIDTH // 256, one, 0)
        row = rows_of(acc_v[rows])
        ins_v[at] = jnp.concatenate([row] * (4 // chunk[2]), axis=0)
        inr_v[at, tp] = ins_v[at]
        for j in range(1, TP):
            inner_copy(chunk, j, tp).start()

    def terms(chunk):
        l, at, rows = chunk[0], index(chunk), tokens(chunk)
        for j in range(1, TP):
            inner_copy(chunk, j, lax.rem(tp - j + TP, TP)).wait_recv()
        total = inr_v[at, 0]
        for i in range(1, TP):
            total = total + inr_v[at, i]
        inv = inv_v[l, rows]
        acc_v[rows] = inv * inv * inv * columns_of(total[0 : 2 * chunk[2], :]) * (1.0 / MODEL)

        def one(n, unused):
            cols = pl.ds(pl.multiple_of(n * 128, 128), 128)
            term = inv_v[l, rows] * ng_v[l % 2, rows, cols] - acc_v[rows] * h_v[l, rows, cols].astype(F32)
            t_v[l, spans(chunk), :, :, cols] = term.astype(BF16).reshape(chunk[2], 2, HALF, 128)
            return unused

        lax.fori_loop(0, WIDTH // 128, one, 0)

    def lora_b_copy(l, j, block, place):
        return remote(lbs_v.at[l, block], lbr_v.at[l, place], lbs_sem.at[l, j - 1], lbr_sem.at[l, j - 1], tp_peer(j))

    def adapters(l):
        inv = inv_v[l][:, :RANK]
        scaled = (2.0 * inv * ad_v[l].astype(F32)).astype(BF16)
        la_v[l] = dot(scaled, h_v[l], ((0,), (0,)))
        low = (2.0 * inv * hd_v[l]).astype(BF16)
        part = dot(low, gathered(l, slice(0, TOKENS)), ((0,), (0,)))
        for j in range(TP):
            lbs_v[l, j] = part[:, 128 * j : 128 * j + 128].astype(BF16)
        lbr_v[l, tp] = lbs_v[l, tp]
        for j in range(1, TP):
            lora_b_copy(l, j, lax.rem(tp + j, TP), tp).start()
        pltpu.make_async_copy(la_v.at[l], la_hbm.at[l], out_sem.at[l]).start()

    def adapters_end(l):
        for j in range(1, TP):
            lora_b_copy(l, j, 0, lax.rem(tp - j + TP, TP)).wait_recv()
        total = lbr_v[l, 0].astype(F32)
        for i in range(1, TP):
            total = total + lbr_v[l, i].astype(F32)
        lb_v[l] = total
        pltpu.make_async_copy(lb_v.at[l], lb_hbm.at[l], out_sem.at[LAYERS + l]).start()

    def core_copy(chunk):
        at = index(chunk)
        return remote(
            t_v.at[chunk[0], spans(chunk), 1 - core], tp_v.at[chunk[0], spans(chunk)],
            cs_sem.at[at], cr_sem.at[at], core_peer,
        )

    def to_owner(chunk, j, place):
        at = index(chunk)
        return remote(
            p_v.at[chunk[0], spans(chunk), chip_index(j)], q8_v.at[chunk[0], place, spans(chunk)],
            p1s_sem.at[at, j - 1], p1r_sem.at[at, j - 1], chip_peer(j),
        )

    def from_owner(chunk, j, place):
        at = index(chunk)
        return remote(
            rs_v.at[chunk[0], chip_index(j), spans(chunk)], rr_v.at[chunk[0], spans(chunk), place],
            p2s_sem.at[at, j - 1], p2r_sem.at[at, j - 1], chip_peer(j),
        )

    def source(j):
        return lax.rem(chip - j + CHIPS, CHIPS)

    def pair_sums(chunk):
        l, ts = chunk[0], spans(chunk)
        core_copy(chunk).wait_recv()
        both = t_v[l, ts, core].astype(F32) + tp_v[l, ts].astype(F32)
        p_v[l, ts] = both.reshape(chunk[2], CHIPS, ROWS, WIDTH).astype(BF16)
        for j in (4, 2, 6, 1, 3, 5, 7):
            to_owner(chunk, j, chip).start()
        q8_v[l, chip, ts] = p_v[l, ts, chip]

    def suffix(chunk):
        l, ts = chunk[0], spans(chunk)
        if l == LAYERS - 1:
            if chunk[1] == 0:
                copies["top"].wait()
            weights = jnp.concatenate([weight_v[ts, core, chip]] * (WIDTH // 128), axis=2)
            carry = weights * top_v[ts].astype(F32)
        else:
            carry = carry_v[ts]
        for j in range(1, CHIPS):
            to_owner(chunk, j, source(j)).wait_recv()
        for i in reversed(range(CHIPS)):
            rs_v[l, i, ts] = carry.astype(BF16)
            carry = carry + q8_v[l, i, ts].astype(F32)
        carry_v[ts] = carry
        for j in (4, 2, 6, 1, 3, 5, 7):
            from_owner(chunk, j, chip).start()
        rr_v[l, ts, chip] = rs_v[l, chip, ts]

    def out_copy(chunk):
        at = index(chunk)
        return remote(
            peer_v.at[chunk[0], spans(chunk)], out_hbm.at[chunk[0], spans(chunk), core],
            os_sem.at[at], or_sem.at[at], core_peer,
        )

    def out_in(chunk):
        at = index(chunk)
        return remote(
            peer_v.at[chunk[0], spans(chunk)], out_hbm.at[chunk[0], spans(chunk), 1 - core],
            os_sem.at[at], or_sem.at[at], core_peer,
        )

    def out_here(chunk):
        return pltpu.make_async_copy(
            own_v.at[chunk[0], spans(chunk)], out_hbm.at[chunk[0], spans(chunk), core], out_sem.at[2 * LAYERS + index(chunk)]
        )

    def finish(chunk):
        l, ts = chunk[0], spans(chunk)
        for j in range(1, CHIPS):
            from_owner(chunk, j, source(j)).wait_recv()
        first = (1 - core).astype(F32)
        second = core.astype(F32)
        carry = rr_v[l, ts].astype(F32).reshape(chunk[2], HALF, WIDTH)
        term = t_v[l, ts, core].astype(F32)
        peer_term = tp_v[l, ts].astype(F32)
        peer_v[l, ts] = (carry + peer_term + second * term).astype(BF16)
        out_copy(chunk).start()
        own_v[l, ts] = (carry + term + first * peer_term).astype(BF16)
        out_here(chunk).start()

    attention(2)
    pl.semaphore_wait(barrier, TP + CHIPS - 1)
    gather_1((2, 0, 2))
    attention(1)
    gather_1((1, 0, 2))
    gather_2((2, 0, 2))
    gather_3((2, 0, 2))
    squares_and_low()
    squares_send()
    gather_2((1, 0, 2))
    gather_4((2, 0, 2))
    attention(0)
    gather_4((1, 0, 2))
    gather_3((1, 0, 2))
    gather_1((0, 0, 2))
    gather_end((2, 0, 2))
    products((2, 0, 2))
    gather_2((0, 0, 2))
    gather_end((1, 0, 2))
    products((1, 0, 2))
    squares_wait()
    terms((2, 0, 2))
    core_copy((2, 0, 2)).start()
    gather_4((0, 0, 2))
    gather_3((0, 0, 2))
    adapters(1)
    pair_sums((2, 0, 2))
    terms((1, 0, 2))
    core_copy((1, 0, 2)).start()
    gather_end((0, 0, 2))
    pair_sums((1, 0, 2))
    products((0, 0, 2))
    suffix((2, 0, 2))
    terms((0, 0, 2))
    adapters(2)
    core_copy((0, 0, 2)).start()
    pair_sums((0, 0, 2))
    suffix((1, 0, 2))
    suffix((0, 0, 2))
    adapters_end(2)
    finish((1, 0, 2))
    adapters(0)
    adapters_end(1)
    finish((2, 0, 2))
    finish((0, 0, 2))
    adapters_end(0)

    for chunk in CHUNKS:
        out_in(chunk).wait_recv()
        out_copy(chunk).wait_send()
        out_here(chunk).wait()
        core_copy(chunk).wait_send()
        for i in range(7):
            gather_out(chunk, i).wait_send()
        for j in range(1, TP):
            inner_copy(chunk, j, tp).wait_send()
        for j in range(1, CHIPS):
            to_owner(chunk, j, chip).wait_send()
            from_owner(chunk, j, chip).wait_send()
    for l in range(LAYERS):
        pltpu.make_async_copy(la_v.at[l], la_hbm.at[l], out_sem.at[l]).wait()
        pltpu.make_async_copy(lb_v.at[l], lb_hbm.at[l], out_sem.at[LAYERS + l]).wait()
        for j in range(1, TP):
            lora_b_copy(l, j, lax.rem(tp + j, TP), tp).wait_send()
    for j in range(1, TP):
        squares_copy(j, tp).wait_send()


def place(grad_ref, a_ref, b_ref, grad_out, a_out, b_out, grad_v, a_v, b_v, in_sem, out_sem):
    pieces = [(a_ref, a_v, a_out), (b_ref, b_v, b_out)]
    for l in range(LAYERS):
        for t in range(2):
            at = (l, t)
            pieces.append((grad_ref.at[at], grad_v.at[at], grad_out.at[at]))
    reads = [pltpu.make_async_copy(src, mid, in_sem.at[i]) for i, (src, mid, _) in enumerate(pieces)]
    writes = [pltpu.make_async_copy(mid, dst, out_sem.at[i]) for i, (_, mid, dst) in enumerate(pieces)]
    for copy in reads:
        copy.start()
    for read, write in zip(reads, writes):
        read.wait()
        write.start()
    for copy in writes:
        copy.wait()


def per_device(
    queries, attention_output_grads, keys, hidden, value_weight, value_down_matrix, value_up_matrix,
    document_index, advantage, loss_token_mask, top_stream_gradient,
):
    hbm = pl.BlockSpec(memory_space=pl.ANY)
    vmem = pl.BlockSpec(memory_space=pltpu.VMEM)
    dma = pltpu.SemaphoreType.DMA
    scratch = [
        pltpu.VMEM((LAYERS, TOKENS, WIDTH), BF16),
        pltpu.VMEM((LAYERS, TOKENS, WIDTH), BF16),
        pltpu.VMEM((LAYERS, TOKENS, HEAD), BF16),
        pltpu.VMEM((LAYERS, TOKENS, WIDTH), BF16),
        pltpu.VMEM((LAYERS, WIDTH, WIDTH), BF16),
        pltpu.VMEM((LAYERS, RANK, WIDTH), BF16),
        pltpu.VMEM((LAYERS, RANK, WIDTH), BF16),
        pltpu.VMEM((2, ROWS, WIDTH), BF16),
        pltpu.VMEM((1152, 128), F32),
        pltpu.VMEM((2, 2, CHIPS, ROWS, 128), F32),
        pltpu.VMEM((TOKENS, 128), F32),
        pltpu.VMEM((LAYERS, TP, TOKENS, HEAD), BF16),
        pltpu.VMEM((LAYERS, TOKENS, RANK), F32),
        pltpu.VMEM((LAYERS, TOKENS, RANK), BF16),
        pltpu.VMEM((2, TOKENS, WIDTH), F32),
        pltpu.VMEM((LAYERS, TOKENS, 128), F32),
        pltpu.VMEM((16, 128), F32),
        pltpu.VMEM((TP, 16, 128), F32),
        pltpu.VMEM((2 * LAYERS, 8, 128), F32),
        pltpu.VMEM((2 * LAYERS, TP, 8, 128), F32),
        pltpu.VMEM((LAYERS, TP, RANK, HEAD), BF16),
        pltpu.VMEM((LAYERS, TP, RANK, HEAD), BF16),
        pltpu.VMEM((LAYERS, RANK, WIDTH), F32),
        pltpu.VMEM((LAYERS, RANK, HEAD), F32),
        pltpu.VMEM((LAYERS, 2, 2, HALF, WIDTH), BF16),
        pltpu.VMEM((LAYERS, 2, HALF, WIDTH), BF16),
        pltpu.VMEM((LAYERS, 2, CHIPS, ROWS, WIDTH), BF16),
        pltpu.VMEM((LAYERS, CHIPS, 2, ROWS, WIDTH), BF16),
        pltpu.VMEM((LAYERS, CHIPS, 2, ROWS, WIDTH), BF16),
        pltpu.VMEM((LAYERS, 2, CHIPS, ROWS, WIDTH), BF16),
        pltpu.VMEM((2, ROWS, WIDTH), F32),
        pltpu.VMEM((LAYERS, 2, HALF, WIDTH), BF16),
        pltpu.VMEM((LAYERS, 2, HALF, WIDTH), BF16),
        dma((16,)), dma((4 * LAYERS,)),
        dma((2 * LAYERS, 7)), dma((2 * LAYERS, 7)), dma((7,)), dma((7,)), dma((2 * LAYERS, 7)), dma((2 * LAYERS, 7)),
        dma((LAYERS, 7)), dma((LAYERS, 7)),
        dma((2 * LAYERS,)), dma((2 * LAYERS,)),
        dma((2 * LAYERS, 7)), dma((2 * LAYERS, 7)), dma((2 * LAYERS, 7)), dma((2 * LAYERS, 7)),
        dma((2 * LAYERS,)), dma((2 * LAYERS,)),
    ]
    grad_in, lora_a, lora_b = pl.pallas_call(
        kernel,
        name="value_backward",
        out_shape=(
            jax.ShapeDtypeStruct((LAYERS, 2, 2, HALF, WIDTH), BF16),
            jax.ShapeDtypeStruct((LAYERS, RANK, WIDTH), F32),
            jax.ShapeDtypeStruct((LAYERS, RANK, HEAD), F32),
        ),
        in_specs=[hbm] * 8 + [vmem] * 3,
        out_specs=(hbm, hbm, hbm),
        scratch_shapes=scratch,
        compiler_params=pltpu.CompilerParams(
            collective_id=0, has_side_effects=True, vmem_limit_bytes=60 << 20
        ),
        cost_estimate=pl.CostEstimate(flops=8_000_000_000, bytes_accessed=22_000_000, transcendentals=4_000_000),
    )(
        queries[0], attention_output_grads[0], keys[0], hidden[0], value_weight[0], jnp.swapaxes(value_down_matrix[0], 1, 2),
        value_up_matrix[0], top_stream_gradient.reshape(2, 2, CHIPS, ROWS, WIDTH),
        document_index.reshape(1, TOKENS), advantage.reshape(1, TOKENS), loss_token_mask.reshape(1, TOKENS),
    )
    grad_in, lora_a, lora_b = pl.pallas_call(
        place,
        name="place",
        out_shape=(
            jax.ShapeDtypeStruct(grad_in.shape, BF16),
            jax.ShapeDtypeStruct(lora_a.shape, F32),
            jax.ShapeDtypeStruct(lora_b.shape, F32),
        ),
        in_specs=[hbm] * 3,
        out_specs=(hbm, hbm, hbm),
        scratch_shapes=[
            pltpu.VMEM(grad_in.shape, BF16),
            pltpu.VMEM(lora_a.shape, F32),
            pltpu.VMEM(lora_b.shape, F32),
            dma((8,)), dma((8,)),
        ],
        compiler_params=pltpu.CompilerParams(vmem_limit_bytes=60 << 20),
    )(grad_in, lora_a, lora_b)
    return grad_in.reshape(1, LAYERS, TOKENS, WIDTH), jnp.swapaxes(lora_a, 1, 2)[None], lora_b[None]


def solution(mesh):
    in_specs = (
        P("pp", None, None, "tp"),
        P("pp", None, None, "tp"),
        P("pp", None, None, "tp"),
        P("pp", None, None, "tp"),
        P("pp", None, "tp", None),
        P("pp", None, "tp", None),
        P("pp", None, None, None),
        P(),
        P(),
        P(),
        P(None, "tp"),
    )
    out_specs = (P("pp", None, None, "tp"), P("pp", None, "tp", None), P("pp", None, None, "tp"))
    return jax.shard_map(
        per_device, mesh=mesh, in_specs=in_specs, out_specs=out_specs, check_vma=False
    )
```

```python
import jax
import jax.numpy as jnp
from jax import lax
from jax.experimental import pallas as pl
from jax.experimental.pallas import tpu as pltpu
from jax.sharding import PartitionSpec as P

MESH = pl.DeviceIdType.MESH
BF16 = jnp.bfloat16
F32 = jnp.float32
LAYERS = 3
TOKENS = 512
WIDTH = 1024
HEAD = 128
HEADS = 8
RANK = 64
SPAN = 256
HALF = 128
ROWS = 32
CHIPS = 4
TP = 8
MODEL = 8192
SEGS = 8
LOG2E = 1.4426950408889634
GATHER_CHUNKS = ((2, 1, 1), (2, 0, 1), (1, 0, 2), (0, 0, 2))
PRODUCT_CHUNKS = ((2, 0, 1), (2, 1, 1), (1, 0, 2), (0, 0, 2))
SUM_CHUNKS = ((2, 0, 1), (0, 0, 1), (2, 1, 1), (1, 0, 2), (0, 1, 1))
SOFTMAX_SCALE = HEAD**-0.5 * LOG2E
MASK_OFFSET = (0, 128, 384, 768)


def dot(a, b, dims):
    return lax.dot_general(a, b, (dims, ((), ())), preferred_element_type=F32)


def kernel(
    q_hbm, g_hbm, k_hbm, h_hbm, w_hbm, dn_hbm, up_hbm, top_hbm, doc_ref, adv_ref, loss_ref,
    out_hbm, la_hbm, lb_hbm,
    q_v, g_v, k_v, h_v, w_v, dn_v, up_v, top_v,
    mask_v, weight_v, acc_v, vg_v, hd_v, ad_v, ng_v, inv_v,
    sqs_v, sqr_v, ins_v, inr_v, lbs_v, lbr_v, la_v, lb_v,
    t_v, tp_v, p_v, q8_v, rs_v, rr_v, carry_v, tots_v, totr_v, own_v, peer_v,
    in_sem, out_sem,
    gs_sem, gr_sem, sqs_sem, sqr_sem, ins_sem, inr_sem, lbs_sem, lbr_sem,
    cs_sem, cr_sem, p1s_sem, p1r_sem, p2s_sem, p2r_sem, hs_sem, hr_sem, os_sem, or_sem,
):
    pp = lax.axis_index("pp")
    tp = lax.axis_index("tp")
    core = lax.rem(pp, 2)
    chip = lax.rem(lax.div(pp, 2), CHIPS)
    half = lax.div(pp, 2 * CHIPS)
    yl = lax.div(tp, 4)
    x = lax.rem(tp, 4)

    yl_peer = (pp, (1 - yl) * 4 + x)
    x_up = (pp, yl * 4 + lax.rem(x + 1, 4))
    x_down = (pp, yl * 4 + lax.rem(x + 3, 4))
    core_peer = (pp + 1 - 2 * core, tp)
    half_peer = (lax.rem(pp + 2 * CHIPS, 4 * CHIPS), tp)

    def tp_peer(j):
        return (pp, lax.rem(tp + j, TP))

    def chip_index(j):
        return lax.rem(chip + j, CHIPS)

    def chip_peer(j):
        return ((half * CHIPS + chip_index(j)) * 2 + core, tp)

    copies = {}

    def load(name, src, dst):
        copies[name] = pltpu.make_async_copy(src, dst, in_sem.at[len(copies)])

    for l in (2, 1, 0):
        load(("k", l), k_hbm.at[l], k_v.at[l])
        load(("q", l), q_hbm.at[l], q_v.at[l])
        load(("g", l), g_hbm.at[l], g_v.at[l])
    load("h", h_hbm, h_v)
    load("dn", dn_hbm, dn_v)
    load("up", up_hbm, up_v)
    for l in (2, 1, 0):
        load(("w", l), w_hbm.at[l], w_v.at[l])
    load("top", top_hbm.at[:, core, chip], top_v)
    first = [(name, LAYERS - 1) for name in "kqg"]
    for name in first:
        copies[name].start()

    barrier = pltpu.get_barrier_semaphore()
    for j in range(1, TP):
        pl.semaphore_signal(barrier, inc=1, device_id=tp_peer(j), device_id_type=MESH)
    for j in range(1, CHIPS):
        pl.semaphore_signal(barrier, inc=1, device_id=chip_peer(j), device_id_type=MESH)
    for peer in (core_peer, half_peer):
        pl.semaphore_signal(barrier, inc=1, device_id=peer, device_id_type=MESH)

    def remote(src, dst, send, recv, device):
        return pltpu.make_async_remote_copy(
            src_ref=src, dst_ref=dst, send_sem=send, recv_sem=recv, device_id=device, device_id_type=MESH
        )

    def columns(row):
        return jnp.transpose(jnp.broadcast_to(row, (128, TOKENS)))

    def rows_of(sums):
        parts = [sums[128 * i : 128 * i + 128, :] for i in range(sums.shape[0] // 128)]
        return jnp.concatenate([jnp.sum(jnp.transpose(part), axis=0, keepdims=True) for part in parts], axis=0)

    def columns_of(rows):
        return jnp.concatenate(
            [jnp.transpose(jnp.broadcast_to(rows[i : i + 1, :], (128, 128))) for i in range(rows.shape[0])], axis=0
        )

    doc_row = doc_ref[...].astype(F32)
    doc_col = columns(doc_row)
    key_pos = lax.broadcasted_iota(jnp.int32, (128, 128), 0)
    query_pos = lax.broadcasted_iota(jnp.int32, (128, 128), 1)
    for b in range(4):
        low = max(0, b - 2)
        for kb in range(low, b + 1):
            allowed = doc_col[128 * kb : 128 * kb + 128, :] == doc_row[:, 128 * b : 128 * b + 128]
            if kb == b:
                allowed = allowed & (key_pos <= query_pos)
            at = MASK_OFFSET[b] + 128 * (kb - low)
            mask_v[at : at + 128, :] = jnp.where(allowed, 0.0, -jnp.inf)
    loss_row = loss_ref[...].astype(F32)
    labels = lax.broadcasted_iota(jnp.int32, (SEGS, TOKENS), 0).astype(F32)
    member = jnp.where(labels == doc_row, 1.0, 0.0)
    counts = jnp.sum(member * loss_row, axis=1, keepdims=True)
    per_token = jnp.sum(member * (1.0 / jnp.maximum(counts, 1.0)), axis=0, keepdims=True)
    weights = columns(adv_ref[...].astype(F32) * loss_row * per_token * (TOKENS / SEGS))
    weight_v[...] = weights.reshape(2, 2, CHIPS, ROWS, 128)

    slot = x * 2 + yl
    other = x * 2 + (1 - yl)
    left = lax.rem(x + 3, 4) * 2
    right = lax.rem(x + 1, 4) * 2
    across = lax.rem(x + 2, 4) * 2

    def attention(l):
        for name in ("k", "q", "g"):
            copies[(name, l)].wait()
        if l == LAYERS - 1:
            for name in copies:
                if name not in first:
                    copies[name].start()
        for b in range(4):
            low, high = max(0, b - 2) * 128, (b + 1) * 128
            keys = k_v[l, low:high, :]
            mask = mask_v[MASK_OFFSET[b] : MASK_OFFSET[b] + high - low, :]
            mask4 = jnp.concatenate([mask] * 4, axis=1)
            total = None
            for part in range(2):
                heads = range(4 * part, 4 * part + 4)
                block = slice(128 * b, 128 * b + 128)
                queries = jnp.concatenate([q_v[l, block, HEAD * i : HEAD * i + HEAD] for i in heads], axis=0)
                grads = jnp.concatenate([g_v[l, block, HEAD * i : HEAD * i + HEAD] for i in heads], axis=0)
                scores = dot(keys, queries, ((1,), (1,))) + mask4
                peak = jnp.max(scores, axis=0, keepdims=True)
                expo = jnp.exp2((scores - peak) * SOFTMAX_SCALE)
                probs = (expo * (1.0 / jnp.sum(expo, axis=0, keepdims=True))).astype(BF16)
                piece = dot(probs, grads, ((1,), (0,)))
                total = piece if total is None else total + piece
            if b == 0:
                acc_v[0:128, :] = total
            else:
                acc_v[low : high - 128, :] += total[: high - low - 128]
                acc_v[high - 128 : high, :] = total[high - low - 128 :]
        vg_v[l, slot] = acc_v[...].astype(BF16)

    def spans(chunk):
        return pl.ds(chunk[1], chunk[2])

    def tokens(chunk):
        return slice(chunk[1] * SPAN, (chunk[1] + chunk[2]) * SPAN)

    def index(chunk):
        return chunk[0] * 2 + chunk[1]

    def gather_copy(chunk, i, place, device):
        part = vg_v.at[chunk[0], place, pl.ds(chunk[1] * SPAN, chunk[2] * SPAN)]
        return remote(part, part, gs_sem.at[index(chunk), i], gr_sem.at[index(chunk), i], device)

    def gather_out(chunk, i):
        return (
            lambda: gather_copy(chunk, 0, slot, yl_peer),
            lambda: gather_copy(chunk, 1, slot, x_up),
            lambda: gather_copy(chunk, 2, slot, x_down),
            lambda: gather_copy(chunk, 3, other, x_up),
            lambda: gather_copy(chunk, 4, other, x_down),
            lambda: gather_copy(chunk, 5, left + yl, x_up),
            lambda: gather_copy(chunk, 6, right + (1 - yl), x_down),
        )[i]()

    def gather_in(chunk, i):
        place = (other, left + yl, right + yl, left + (1 - yl), right + (1 - yl), across + yl, across + (1 - yl))[i]
        return gather_copy(chunk, i, place, yl_peer)

    def gather_1(chunk):
        for i in (0, 1, 2):
            gather_out(chunk, i).start()

    def gather_2(chunk):
        gather_in(chunk, 0).wait_recv()
        for i in (3, 4):
            gather_out(chunk, i).start()

    def gather_3(chunk):
        gather_in(chunk, 1).wait_recv()
        gather_out(chunk, 5).start()

    def gather_4(chunk):
        gather_in(chunk, 4).wait_recv()
        gather_out(chunk, 6).start()

    def gather_end(chunk):
        for i in (2, 3, 5, 6):
            gather_in(chunk, i).wait_recv()

    def squares_and_low():
        sqs_v[...] = jnp.zeros((16, 128), F32)
        copies["h"].wait()
        copies["dn"].wait()
        for l in range(LAYERS):
            sums = None
            for n in range(WIDTH // 128):
                part = h_v[l, :, 128 * n : 128 * n + 128].astype(F32)
                sums = part * part if sums is None else sums + part * part
            sqs_v[4 * l : 4 * l + 4, :] = rows_of(sums)
            hd_v[l] = dot(h_v[l], dn_v[l], ((1,), (1,)))
        sqr_v[tp] = sqs_v[...]

    def squares_copy(j, place):
        return remote(sqs_v, sqr_v.at[place], sqs_sem.at[j - 1], sqr_sem.at[j - 1], tp_peer(j))

    def squares_send():
        for j in range(1, TP):
            squares_copy(j, tp).start()

    def squares_wait():
        for j in range(1, TP):
            squares_copy(j, lax.rem(tp - j + TP, TP)).wait_recv()
        total = sqr_v[0]
        for i in range(1, TP):
            total = total + sqr_v[i]
        inverse = lax.rsqrt(total * (1.0 / MODEL) + 1e-5)
        for l in range(LAYERS):
            inv_v[l] = columns_of(inverse[4 * l : 4 * l + 4, :])

    def gathered(l, rows):
        return jnp.concatenate([vg_v[l, (j % 4) * 2 + j // 4, rows] for j in range(TP)], axis=1)

    def inner_copy(chunk, j, place):
        at = index(chunk)
        return remote(ins_v.at[at], inr_v.at[at, place], ins_sem.at[at, j - 1], inr_sem.at[at, j - 1], tp_peer(j))

    def products(chunk):
        l, at, rows = chunk[0], index(chunk), tokens(chunk)
        if l == LAYERS - 1 and chunk[1] == 0:
            copies["up"].wait()
        if chunk[1] == 0:
            copies[("w", l)].wait()
        ad_v[l, rows] = dot(gathered(l, rows), up_v[l], ((1,), (1,))).astype(BF16)
        acc_v[rows] = jnp.zeros((chunk[2] * SPAN, 128), F32)

        def one(n, unused):
            cols = pl.ds(pl.multiple_of(n * 256, 256), 256)
            twice = (ad_v[l, rows].astype(F32) * 2.0).astype(BF16)
            ng = dot(gathered(l, rows), w_v[l, cols, :], ((1,), (1,))) + dot(twice, dn_v[l, :, cols], ((1,), (0,)))
            ng_v[l % 2, rows, cols] = ng
            prod = h_v[l, rows, cols].astype(F32) * ng
            acc_v[rows] += prod[:, :128] + prod[:, 128:]
            return unused

        lax.fori_loop(0, WIDTH // 256, one, 0)
        row = rows_of(acc_v[rows])
        ins_v[at] = jnp.concatenate([row] * (4 // chunk[2]), axis=0)
        inr_v[at, tp] = ins_v[at]
        for j in range(1, TP):
            inner_copy(chunk, j, tp).start()

    def terms(chunk):
        l, at, rows = chunk[0], index(chunk), tokens(chunk)
        for j in range(1, TP):
            inner_copy(chunk, j, lax.rem(tp - j + TP, TP)).wait_recv()
        total = inr_v[at, 0]
        for i in range(1, TP):
            total = total + inr_v[at, i]
        inv = inv_v[l, rows]
        acc_v[rows] = inv * inv * inv * columns_of(total[0 : 2 * chunk[2], :]) * (1.0 / MODEL)

        def one(n, unused):
            cols = pl.ds(pl.multiple_of(n * 128, 128), 128)
            term = inv_v[l, rows] * ng_v[l % 2, rows, cols] - acc_v[rows] * h_v[l, rows, cols].astype(F32)
            t_v[l, spans(chunk), :, :, cols] = term.astype(BF16).reshape(chunk[2], 2, HALF, 128)
            return unused

        lax.fori_loop(0, WIDTH // 128, one, 0)

    def lora_b_copy(l, j, block, place):
        return remote(lbs_v.at[l, block], lbr_v.at[l, place], lbs_sem.at[l, j - 1], lbr_sem.at[l, j - 1], tp_peer(j))

    def adapters(l):
        inv = inv_v[l][:, :RANK]
        scaled = (2.0 * inv * ad_v[l].astype(F32)).astype(BF16)
        la_v[l] = dot(scaled, h_v[l], ((0,), (0,)))
        low = (2.0 * inv * hd_v[l]).astype(BF16)
        part = dot(low, gathered(l, slice(0, TOKENS)), ((0,), (0,)))
        for j in range(TP):
            lbs_v[l, j] = part[:, 128 * j : 128 * j + 128].astype(BF16)
        lbr_v[l, tp] = lbs_v[l, tp]
        for j in range(1, TP):
            lora_b_copy(l, j, lax.rem(tp + j, TP), tp).start()
        pltpu.make_async_copy(la_v.at[l], la_hbm.at[l], out_sem.at[l]).start()

    def adapters_end(l):
        for j in range(1, TP):
            lora_b_copy(l, j, 0, lax.rem(tp - j + TP, TP)).wait_recv()
        total = lbr_v[l, 0].astype(F32)
        for i in range(1, TP):
            total = total + lbr_v[l, i].astype(F32)
        lb_v[l] = total
        pltpu.make_async_copy(lb_v.at[l], lb_hbm.at[l], out_sem.at[LAYERS + l]).start()

    def core_copy(chunk):
        at = index(chunk)
        return remote(
            t_v.at[chunk[0], spans(chunk), 1 - core], tp_v.at[chunk[0], spans(chunk)],
            cs_sem.at[at], cr_sem.at[at], core_peer,
        )

    def to_owner(chunk, j, place):
        at = index(chunk)
        return remote(
            p_v.at[chunk[0], spans(chunk), chip_index(j)], q8_v.at[chunk[0], place, spans(chunk)],
            p1s_sem.at[at, j - 1], p1r_sem.at[at, j - 1], chip_peer(j),
        )

    def from_owner(chunk, j, place):
        at = index(chunk)
        return remote(
            rs_v.at[chunk[0], chip_index(j), spans(chunk)], rr_v.at[chunk[0], spans(chunk), place],
            p2s_sem.at[at, j - 1], p2r_sem.at[at, j - 1], chip_peer(j),
        )

    def source(j):
        return lax.rem(chip - j + CHIPS, CHIPS)

    def pair_sums(chunk):
        l, ts = chunk[0], spans(chunk)
        core_copy(chunk).wait_recv()
        both = t_v[l, ts, core].astype(F32) + tp_v[l, ts].astype(F32)
        p_v[l, ts] = both.reshape(chunk[2], CHIPS, ROWS, WIDTH).astype(BF16)
        for j in (2, 1, 3):
            to_owner(chunk, j, chip).start()
        q8_v[l, chip, ts] = p_v[l, ts, chip]

    def total_copy(chunk):
        at = index(chunk)
        return remote(
            tots_v.at[chunk[0], spans(chunk)], totr_v.at[chunk[0], spans(chunk)],
            hs_sem.at[at], hr_sem.at[at], half_peer,
        )

    def totals(chunk):
        l, ts = chunk[0], spans(chunk)
        for j in range(1, CHIPS):
            to_owner(chunk, j, source(j)).wait_recv()
        total = q8_v[l, 0, ts].astype(F32)
        for i in range(1, CHIPS):
            total = total + q8_v[l, i, ts].astype(F32)
        tots_v[l, ts] = total.astype(BF16)
        total_copy(chunk).start()

    def suffix(chunk):
        l, ts = chunk[0], spans(chunk)
        if l == LAYERS - 1:
            if chunk[1] == 0:
                copies["top"].wait()
            weights = jnp.concatenate([weight_v[ts, core, chip]] * (WIDTH // 128), axis=2)
            carry = weights * top_v[ts].astype(F32)
        else:
            carry = carry_v[ts]
        total_copy(chunk).wait_recv()
        above = totr_v[l, ts].astype(F32)
        carry_v[ts] = carry + above + tots_v[l, ts].astype(F32)
        carry = carry + (1 - half).astype(F32) * above
        for i in reversed(range(CHIPS)):
            rs_v[l, i, ts] = carry.astype(BF16)
            carry = carry + q8_v[l, i, ts].astype(F32)
        for j in (2, 1, 3):
            from_owner(chunk, j, chip).start()
        rr_v[l, ts, chip] = rs_v[l, chip, ts]

    def out_copy(chunk):
        at = index(chunk)
        return remote(
            peer_v.at[chunk[0], spans(chunk)], out_hbm.at[chunk[0], spans(chunk), core],
            os_sem.at[at], or_sem.at[at], core_peer,
        )

    def out_in(chunk):
        at = index(chunk)
        return remote(
            peer_v.at[chunk[0], spans(chunk)], out_hbm.at[chunk[0], spans(chunk), 1 - core],
            os_sem.at[at], or_sem.at[at], core_peer,
        )

    def out_here(chunk):
        return pltpu.make_async_copy(
            own_v.at[chunk[0], spans(chunk)], out_hbm.at[chunk[0], spans(chunk), core], out_sem.at[2 * LAYERS + index(chunk)]
        )

    def finish(chunk):
        l, ts = chunk[0], spans(chunk)
        for j in range(1, CHIPS):
            from_owner(chunk, j, source(j)).wait_recv()
        first = (1 - core).astype(F32)
        second = core.astype(F32)
        carry = rr_v[l, ts].astype(F32).reshape(chunk[2], HALF, WIDTH)
        term = t_v[l, ts, core].astype(F32)
        peer_term = tp_v[l, ts].astype(F32)
        peer_v[l, ts] = (carry + peer_term + second * term).astype(BF16)
        out_copy(chunk).start()
        own_v[l, ts] = (carry + term + first * peer_term).astype(BF16)
        out_here(chunk).start()

    attention(2)
    pl.semaphore_wait(barrier, TP + CHIPS)
    gather_1((2, 1, 1))
    gather_1((2, 0, 1))
    attention(1)
    gather_1((1, 0, 2))
    gather_2((2, 1, 1))
    squares_and_low()
    squares_send()
    gather_3((2, 0, 1))
    gather_2((2, 0, 1))
    attention(0)
    gather_2((1, 0, 2))
    gather_4((2, 0, 1))
    squares_wait()
    gather_3((2, 1, 1))
    gather_4((2, 1, 1))
    gather_3((1, 0, 2))
    gather_4((1, 0, 2))
    gather_1((0, 0, 2))
    gather_end((2, 0, 1))
    products((2, 0, 1))
    gather_end((2, 1, 1))
    products((2, 1, 1))
    gather_end((1, 0, 2))
    gather_2((0, 0, 2))
    products((1, 0, 2))
    gather_3((0, 0, 2))
    terms((2, 0, 1))
    core_copy((2, 0, 1)).start()
    terms((2, 1, 1))
    pair_sums((2, 0, 1))
    gather_4((0, 0, 2))
    core_copy((2, 1, 1)).start()
    pair_sums((2, 1, 1))
    terms((1, 0, 2))
    core_copy((1, 0, 2)).start()
    adapters(2)
    pair_sums((1, 0, 2))
    gather_end((0, 0, 2))
    totals((2, 0, 1))
    products((0, 0, 2))
    totals((2, 1, 1))
    suffix((2, 0, 1))
    adapters(0)
    suffix((2, 1, 1))
    terms((0, 0, 2))
    core_copy((0, 0, 1)).start()
    totals((1, 0, 2))
    adapters(1)
    adapters_end(2)
    pair_sums((0, 0, 1))
    core_copy((0, 1, 1)).start()
    pair_sums((0, 1, 1))
    suffix((1, 0, 2))
    totals((0, 0, 1))
    finish((2, 0, 1))
    totals((0, 1, 1))
    suffix((0, 0, 1))
    suffix((0, 1, 1))
    finish((0, 0, 1))
    adapters_end(0)
    adapters_end(1)
    finish((2, 1, 1))
    finish((1, 0, 2))
    finish((0, 1, 1))

    for chunk in GATHER_CHUNKS:
        for i in range(7):
            gather_out(chunk, i).wait_send()
    for chunk in PRODUCT_CHUNKS:
        for j in range(1, TP):
            inner_copy(chunk, j, tp).wait_send()
    for chunk in SUM_CHUNKS:
        out_in(chunk).wait_recv()
        out_copy(chunk).wait_send()
        out_here(chunk).wait()
        core_copy(chunk).wait_send()
        total_copy(chunk).wait_send()
        for j in range(1, CHIPS):
            to_owner(chunk, j, chip).wait_send()
            from_owner(chunk, j, chip).wait_send()
    for l in range(LAYERS):
        pltpu.make_async_copy(la_v.at[l], la_hbm.at[l], out_sem.at[l]).wait()
        pltpu.make_async_copy(lb_v.at[l], lb_hbm.at[l], out_sem.at[LAYERS + l]).wait()
        for j in range(1, TP):
            lora_b_copy(l, j, lax.rem(tp + j, TP), tp).wait_send()
    for j in range(1, TP):
        squares_copy(j, tp).wait_send()


def place(grad_ref, a_ref, b_ref, grad_out, a_out, b_out, grad_v, a_v, b_v, in_sem, out_sem):
    pieces = [(a_ref, a_v, a_out), (b_ref, b_v, b_out)]
    for l in range(LAYERS):
        for t in range(2):
            at = (l, t)
            pieces.append((grad_ref.at[at], grad_v.at[at], grad_out.at[at]))
    reads = [pltpu.make_async_copy(src, mid, in_sem.at[i]) for i, (src, mid, _) in enumerate(pieces)]
    writes = [pltpu.make_async_copy(mid, dst, out_sem.at[i]) for i, (_, mid, dst) in enumerate(pieces)]
    for copy in reads:
        copy.start()
    for read, write in zip(reads, writes):
        read.wait()
        write.start()
    for copy in writes:
        copy.wait()


def per_device(
    queries, attention_output_grads, keys, hidden, value_weight, value_down_matrix, value_up_matrix,
    document_index, advantage, loss_token_mask, top_stream_gradient,
):
    hbm = pl.BlockSpec(memory_space=pl.ANY)
    vmem = pl.BlockSpec(memory_space=pltpu.VMEM)
    dma = pltpu.SemaphoreType.DMA
    scratch = [
        pltpu.VMEM((LAYERS, TOKENS, WIDTH), BF16),
        pltpu.VMEM((LAYERS, TOKENS, WIDTH), BF16),
        pltpu.VMEM((LAYERS, TOKENS, HEAD), BF16),
        pltpu.VMEM((LAYERS, TOKENS, WIDTH), BF16),
        pltpu.VMEM((LAYERS, WIDTH, WIDTH), BF16),
        pltpu.VMEM((LAYERS, RANK, WIDTH), BF16),
        pltpu.VMEM((LAYERS, RANK, WIDTH), BF16),
        pltpu.VMEM((2, ROWS, WIDTH), BF16),
        pltpu.VMEM((1152, 128), F32),
        pltpu.VMEM((2, 2, CHIPS, ROWS, 128), F32),
        pltpu.VMEM((TOKENS, 128), F32),
        pltpu.VMEM((LAYERS, TP, TOKENS, HEAD), BF16),
        pltpu.VMEM((LAYERS, TOKENS, RANK), F32),
        pltpu.VMEM((LAYERS, TOKENS, RANK), BF16),
        pltpu.VMEM((2, TOKENS, WIDTH), F32),
        pltpu.VMEM((LAYERS, TOKENS, 128), F32),
        pltpu.VMEM((16, 128), F32),
        pltpu.VMEM((TP, 16, 128), F32),
        pltpu.VMEM((2 * LAYERS, 8, 128), F32),
        pltpu.VMEM((2 * LAYERS, TP, 8, 128), F32),
        pltpu.VMEM((LAYERS, TP, RANK, HEAD), BF16),
        pltpu.VMEM((LAYERS, TP, RANK, HEAD), BF16),
        pltpu.VMEM((LAYERS, RANK, WIDTH), F32),
        pltpu.VMEM((LAYERS, RANK, HEAD), F32),
        pltpu.VMEM((LAYERS, 2, 2, HALF, WIDTH), BF16),
        pltpu.VMEM((LAYERS, 2, HALF, WIDTH), BF16),
        pltpu.VMEM((LAYERS, 2, CHIPS, ROWS, WIDTH), BF16),
        pltpu.VMEM((LAYERS, CHIPS, 2, ROWS, WIDTH), BF16),
        pltpu.VMEM((LAYERS, CHIPS, 2, ROWS, WIDTH), BF16),
        pltpu.VMEM((LAYERS, 2, CHIPS, ROWS, WIDTH), BF16),
        pltpu.VMEM((2, ROWS, WIDTH), F32),
        pltpu.VMEM((LAYERS, 2, ROWS, WIDTH), BF16),
        pltpu.VMEM((LAYERS, 2, ROWS, WIDTH), BF16),
        pltpu.VMEM((LAYERS, 2, HALF, WIDTH), BF16),
        pltpu.VMEM((LAYERS, 2, HALF, WIDTH), BF16),
        dma((16,)), dma((4 * LAYERS,)),
        dma((2 * LAYERS, 7)), dma((2 * LAYERS, 7)), dma((7,)), dma((7,)), dma((2 * LAYERS, 7)), dma((2 * LAYERS, 7)),
        dma((LAYERS, 7)), dma((LAYERS, 7)),
        dma((2 * LAYERS,)), dma((2 * LAYERS,)),
        dma((2 * LAYERS, 7)), dma((2 * LAYERS, 7)), dma((2 * LAYERS, 7)), dma((2 * LAYERS, 7)),
        dma((2 * LAYERS,)), dma((2 * LAYERS,)),
        dma((2 * LAYERS,)), dma((2 * LAYERS,)),
    ]
    grad_in, lora_a, lora_b = pl.pallas_call(
        kernel,
        name="value_backward",
        out_shape=(
            jax.ShapeDtypeStruct((LAYERS, 2, 2, HALF, WIDTH), BF16),
            jax.ShapeDtypeStruct((LAYERS, RANK, WIDTH), F32),
            jax.ShapeDtypeStruct((LAYERS, RANK, HEAD), F32),
        ),
        in_specs=[hbm] * 8 + [vmem] * 3,
        out_specs=(hbm, hbm, hbm),
        scratch_shapes=scratch,
        compiler_params=pltpu.CompilerParams(
            collective_id=0, has_side_effects=True, vmem_limit_bytes=60 << 20
        ),
        cost_estimate=pl.CostEstimate(flops=8_000_000_000, bytes_accessed=22_000_000, transcendentals=4_000_000),
    )(
        queries[0], attention_output_grads[0], keys[0], hidden[0], value_weight[0], jnp.swapaxes(value_down_matrix[0], 1, 2),
        value_up_matrix[0], top_stream_gradient.reshape(2, 2, CHIPS, ROWS, WIDTH),
        document_index.reshape(1, TOKENS), advantage.reshape(1, TOKENS), loss_token_mask.reshape(1, TOKENS),
    )
    grad_in, lora_a, lora_b = pl.pallas_call(
        place,
        name="place",
        out_shape=(
            jax.ShapeDtypeStruct(grad_in.shape, BF16),
            jax.ShapeDtypeStruct(lora_a.shape, F32),
            jax.ShapeDtypeStruct(lora_b.shape, F32),
        ),
        in_specs=[hbm] * 3,
        out_specs=(hbm, hbm, hbm),
        scratch_shapes=[
            pltpu.VMEM(grad_in.shape, BF16),
            pltpu.VMEM(lora_a.shape, F32),
            pltpu.VMEM(lora_b.shape, F32),
            dma((8,)), dma((8,)),
        ],
        compiler_params=pltpu.CompilerParams(vmem_limit_bytes=60 << 20),
    )(grad_in, lora_a, lora_b)
    return grad_in.reshape(1, LAYERS, TOKENS, WIDTH), jnp.swapaxes(lora_a, 1, 2)[None], lora_b[None]


def solution(mesh):
    in_specs = (
        P("pp", None, None, "tp"),
        P("pp", None, None, "tp"),
        P("pp", None, None, "tp"),
        P("pp", None, None, "tp"),
        P("pp", None, "tp", None),
        P("pp", None, "tp", None),
        P("pp", None, None, None),
        P(),
        P(),
        P(),
        P(None, "tp"),
    )
    out_specs = (P("pp", None, None, "tp"), P("pp", None, "tp", None), P("pp", None, None, "tp"))
    return jax.shard_map(
        per_device, mesh=mesh, in_specs=in_specs, out_specs=out_specs, check_vma=False
    )
```

```python
import jax
import jax.numpy as jnp
from jax import lax
from jax.experimental import pallas as pl
from jax.experimental.pallas import tpu as pltpu
from jax.sharding import PartitionSpec as P

MESH = pl.DeviceIdType.MESH
BF16 = jnp.bfloat16
F32 = jnp.float32
LAYERS = 3
TOKENS = 512
WIDTH = 1024
HEAD = 128
HEADS = 8
RANK = 64
SPAN = 256
HALF = 128
ROWS = 32
CHIPS = 4
TP = 8
MODEL = 8192
SEGS = 8
LOG2E = 1.4426950408889634
GATHER_CHUNKS = ((2, 0, 1), (2, 1, 1), (1, 1, 1), (1, 0, 1), (0, 0, 1), (0, 1, 1))
PRODUCT_CHUNKS = ((2, 0, 1), (2, 1, 1), (1, 0, 1), (1, 1, 1), (0, 0, 1), (0, 1, 1))
SUM_CHUNKS = ((2, 0, 1), (2, 1, 1), (1, 1, 1), (1, 0, 1), (0, 0, 1), (0, 1, 1))
SOFTMAX_SCALE = HEAD**-0.5 * LOG2E
MASK_OFFSET = (0, 128, 384, 768)


def dot(a, b, dims):
    return lax.dot_general(a, b, (dims, ((), ())), preferred_element_type=F32)


def kernel(
    q_hbm, g_hbm, k_hbm, h_hbm, w_hbm, dn_hbm, up_hbm, top_hbm, doc_ref, adv_ref, loss_ref,
    out_hbm, la_hbm, lb_hbm,
    q_v, g_v, k_v, h_v, w_v, dn_v, up_v, top_v,
    mask_v, weight_v, acc_v, vg_v, hd_v, ad_v, ng_v, inv_v,
    sqs_v, sqr_v, ins_v, inr_v, lbs_v, lbr_v, la_v, lb_v,
    t_v, tp_v, p_v, q8_v, rs_v, rr_v, carry_v, tots_v, totr_v, own_v, peer_v,
    in_sem, out_sem,
    gs_sem, gr_sem, sqs_sem, sqr_sem, ins_sem, inr_sem, lbs_sem, lbr_sem,
    cs_sem, cr_sem, p1s_sem, p1r_sem, p2s_sem, p2r_sem, hs_sem, hr_sem, os_sem, or_sem,
):
    pp = lax.axis_index("pp")
    tp = lax.axis_index("tp")
    core = lax.rem(pp, 2)
    chip = lax.rem(lax.div(pp, 2), CHIPS)
    half = lax.div(pp, 2 * CHIPS)
    yl = lax.div(tp, 4)
    x = lax.rem(tp, 4)

    yl_peer = (pp, (1 - yl) * 4 + x)
    x_up = (pp, yl * 4 + lax.rem(x + 1, 4))
    x_down = (pp, yl * 4 + lax.rem(x + 3, 4))
    core_peer = (pp + 1 - 2 * core, tp)
    half_peer = (lax.rem(pp + 2 * CHIPS, 4 * CHIPS), tp)

    def tp_peer(j):
        return (pp, lax.rem(tp + j, TP))

    def chip_index(j):
        return lax.rem(chip + j, CHIPS)

    def chip_peer(j):
        return ((half * CHIPS + chip_index(j)) * 2 + core, tp)

    copies = {}

    def load(name, src, dst):
        copies[name] = pltpu.make_async_copy(src, dst, in_sem.at[len(copies)])

    for l in (2, 1, 0):
        load(("k", l), k_hbm.at[l], k_v.at[l])
        load(("q", l), q_hbm.at[l], q_v.at[l])
        load(("g", l), g_hbm.at[l], g_v.at[l])
    load("h", h_hbm, h_v)
    load("dn", dn_hbm, dn_v)
    load("up", up_hbm, up_v)
    for l in (2, 1, 0):
        load(("w", l), w_hbm.at[l], w_v.at[l])
    load("top", top_hbm.at[:, core, chip], top_v)
    first = [(name, LAYERS - 1) for name in "kqg"]
    for name in first:
        copies[name].start()

    barrier = pltpu.get_barrier_semaphore()
    for j in range(1, TP):
        pl.semaphore_signal(barrier, inc=1, device_id=tp_peer(j), device_id_type=MESH)
    for j in range(1, CHIPS):
        pl.semaphore_signal(barrier, inc=1, device_id=chip_peer(j), device_id_type=MESH)
    for peer in (core_peer, half_peer):
        pl.semaphore_signal(barrier, inc=1, device_id=peer, device_id_type=MESH)

    def remote(src, dst, send, recv, device):
        return pltpu.make_async_remote_copy(
            src_ref=src, dst_ref=dst, send_sem=send, recv_sem=recv, device_id=device, device_id_type=MESH
        )

    def columns(row):
        return jnp.transpose(jnp.broadcast_to(row, (128, TOKENS)))

    def rows_of(sums):
        parts = [sums[128 * i : 128 * i + 128, :] for i in range(sums.shape[0] // 128)]
        return jnp.concatenate([jnp.sum(jnp.transpose(part), axis=0, keepdims=True) for part in parts], axis=0)

    def columns_of(rows):
        return jnp.concatenate(
            [jnp.transpose(jnp.broadcast_to(rows[i : i + 1, :], (128, 128))) for i in range(rows.shape[0])], axis=0
        )

    doc_row = doc_ref[...].astype(F32)
    doc_col = columns(doc_row)
    key_pos = lax.broadcasted_iota(jnp.int32, (128, 128), 0)
    query_pos = lax.broadcasted_iota(jnp.int32, (128, 128), 1)
    for b in range(4):
        low = max(0, b - 2)
        for kb in range(low, b + 1):
            allowed = doc_col[128 * kb : 128 * kb + 128, :] == doc_row[:, 128 * b : 128 * b + 128]
            if kb == b:
                allowed = allowed & (key_pos <= query_pos)
            at = MASK_OFFSET[b] + 128 * (kb - low)
            mask_v[at : at + 128, :] = jnp.where(allowed, 0.0, -jnp.inf)
    loss_row = loss_ref[...].astype(F32)
    labels = lax.broadcasted_iota(jnp.int32, (SEGS, TOKENS), 0).astype(F32)
    member = jnp.where(labels == doc_row, 1.0, 0.0)
    counts = jnp.sum(member * loss_row, axis=1, keepdims=True)
    per_token = jnp.sum(member * (1.0 / jnp.maximum(counts, 1.0)), axis=0, keepdims=True)
    weights = columns(adv_ref[...].astype(F32) * loss_row * per_token * (TOKENS / SEGS))
    weight_v[...] = weights.reshape(2, 2, CHIPS, ROWS, 128)

    slot = x * 2 + yl
    other = x * 2 + (1 - yl)
    left = lax.rem(x + 3, 4) * 2
    right = lax.rem(x + 1, 4) * 2
    across = lax.rem(x + 2, 4) * 2

    def attention(l):
        for name in ("k", "q", "g"):
            copies[(name, l)].wait()
        if l == LAYERS - 1:
            for name in copies:
                if name not in first:
                    copies[name].start()
        for b in range(4):
            low, high = max(0, b - 2) * 128, (b + 1) * 128
            keys = k_v[l, low:high, :]
            mask = mask_v[MASK_OFFSET[b] : MASK_OFFSET[b] + high - low, :]
            mask4 = jnp.concatenate([mask] * 4, axis=1)
            total = None
            for part in range(2):
                heads = range(4 * part, 4 * part + 4)
                block = slice(128 * b, 128 * b + 128)
                queries = jnp.concatenate([q_v[l, block, HEAD * i : HEAD * i + HEAD] for i in heads], axis=0)
                grads = jnp.concatenate([g_v[l, block, HEAD * i : HEAD * i + HEAD] for i in heads], axis=0)
                scores = dot(keys, queries, ((1,), (1,))) + mask4
                peak = jnp.max(scores, axis=0, keepdims=True)
                expo = jnp.exp2((scores - peak) * SOFTMAX_SCALE)
                probs = (expo * (1.0 / jnp.sum(expo, axis=0, keepdims=True))).astype(BF16)
                piece = dot(probs, grads, ((1,), (0,)))
                total = piece if total is None else total + piece
            if b == 0:
                acc_v[0:128, :] = total
            else:
                acc_v[low : high - 128, :] += total[: high - low - 128]
                acc_v[high - 128 : high, :] = total[high - low - 128 :]
        vg_v[l, slot] = acc_v[...].astype(BF16)

    def spans(chunk):
        return pl.ds(chunk[1], chunk[2])

    def tokens(chunk):
        return slice(chunk[1] * SPAN, (chunk[1] + chunk[2]) * SPAN)

    def index(chunk):
        return chunk[0] * 2 + chunk[1]

    def gather_copy(chunk, i, place, device):
        part = vg_v.at[chunk[0], place, pl.ds(chunk[1] * SPAN, chunk[2] * SPAN)]
        return remote(part, part, gs_sem.at[index(chunk), i], gr_sem.at[index(chunk), i], device)

    def gather_out(chunk, i):
        return (
            lambda: gather_copy(chunk, 0, slot, yl_peer),
            lambda: gather_copy(chunk, 1, slot, x_up),
            lambda: gather_copy(chunk, 2, slot, x_down),
            lambda: gather_copy(chunk, 3, other, x_up),
            lambda: gather_copy(chunk, 4, other, x_down),
            lambda: gather_copy(chunk, 5, left + yl, x_up),
            lambda: gather_copy(chunk, 6, right + (1 - yl), x_down),
        )[i]()

    def gather_in(chunk, i):
        place = (other, left + yl, right + yl, left + (1 - yl), right + (1 - yl), across + yl, across + (1 - yl))[i]
        return gather_copy(chunk, i, place, yl_peer)

    def gather_1(chunk):
        for i in (0, 1, 2):
            gather_out(chunk, i).start()

    def gather_2(chunk):
        gather_in(chunk, 0).wait_recv()
        for i in (3, 4):
            gather_out(chunk, i).start()

    def gather_3(chunk):
        gather_in(chunk, 1).wait_recv()
        gather_out(chunk, 5).start()

    def gather_4(chunk):
        gather_in(chunk, 4).wait_recv()
        gather_out(chunk, 6).start()

    def gather_end(chunk):
        for i in (2, 3, 5, 6):
            gather_in(chunk, i).wait_recv()

    def squares_and_low():
        sqs_v[...] = jnp.zeros((16, 128), F32)
        copies["h"].wait()
        copies["dn"].wait()
        for l in range(LAYERS):
            sums = None
            for n in range(WIDTH // 128):
                part = h_v[l, :, 128 * n : 128 * n + 128].astype(F32)
                sums = part * part if sums is None else sums + part * part
            sqs_v[4 * l : 4 * l + 4, :] = rows_of(sums)
            hd_v[l] = dot(h_v[l], dn_v[l], ((1,), (1,)))
        sqr_v[tp] = sqs_v[...]

    def squares_copy(j, place):
        return remote(sqs_v, sqr_v.at[place], sqs_sem.at[j - 1], sqr_sem.at[j - 1], tp_peer(j))

    def squares_send():
        for j in range(1, TP):
            squares_copy(j, tp).start()

    def squares_wait():
        for j in range(1, TP):
            squares_copy(j, lax.rem(tp - j + TP, TP)).wait_recv()
        total = sqr_v[0]
        for i in range(1, TP):
            total = total + sqr_v[i]
        inverse = lax.rsqrt(total * (1.0 / MODEL) + 1e-5)
        for l in range(LAYERS):
            inv_v[l] = columns_of(inverse[4 * l : 4 * l + 4, :])

    def gathered(l, rows):
        return jnp.concatenate([vg_v[l, (j % 4) * 2 + j // 4, rows] for j in range(TP)], axis=1)

    def inner_copy(chunk, j, place):
        at = index(chunk)
        return remote(ins_v.at[at], inr_v.at[at, place], ins_sem.at[at, j - 1], inr_sem.at[at, j - 1], tp_peer(j))

    def products(chunk):
        l, at, rows = chunk[0], index(chunk), tokens(chunk)
        if l == LAYERS - 1 and chunk[1] == 0:
            copies["up"].wait()
        if chunk[1] == 0:
            copies[("w", l)].wait()
        ad_v[l, rows] = dot(gathered(l, rows), up_v[l], ((1,), (1,))).astype(BF16)
        acc_v[rows] = jnp.zeros((chunk[2] * SPAN, 128), F32)

        def one(n, unused):
            cols = pl.ds(pl.multiple_of(n * 256, 256), 256)
            twice = (ad_v[l, rows].astype(F32) * 2.0).astype(BF16)
            ng = dot(gathered(l, rows), w_v[l, cols, :], ((1,), (1,))) + dot(twice, dn_v[l, :, cols], ((1,), (0,)))
            ng_v[l % 2, rows, cols] = ng
            prod = h_v[l, rows, cols].astype(F32) * ng
            acc_v[rows] += prod[:, :128] + prod[:, 128:]
            return unused

        lax.fori_loop(0, WIDTH // 256, one, 0)
        row = rows_of(acc_v[rows])
        ins_v[at] = jnp.concatenate([row] * (4 // chunk[2]), axis=0)
        inr_v[at, tp] = ins_v[at]
        for j in range(1, TP):
            inner_copy(chunk, j, tp).start()

    def terms(chunk):
        l, at, rows = chunk[0], index(chunk), tokens(chunk)
        for j in range(1, TP):
            inner_copy(chunk, j, lax.rem(tp - j + TP, TP)).wait_recv()
        total = inr_v[at, 0]
        for i in range(1, TP):
            total = total + inr_v[at, i]
        inv = inv_v[l, rows]
        acc_v[rows] = inv * inv * inv * columns_of(total[0 : 2 * chunk[2], :]) * (1.0 / MODEL)

        def one(n, unused):
            cols = pl.ds(pl.multiple_of(n * 128, 128), 128)
            term = inv_v[l, rows] * ng_v[l % 2, rows, cols] - acc_v[rows] * h_v[l, rows, cols].astype(F32)
            t_v[l, spans(chunk), :, :, cols] = term.astype(BF16).reshape(chunk[2], 2, HALF, 128)
            return unused

        lax.fori_loop(0, WIDTH // 128, one, 0)

    def lora_b_copy(l, j, block, place):
        return remote(lbs_v.at[l, block], lbr_v.at[l, place], lbs_sem.at[l, j - 1], lbr_sem.at[l, j - 1], tp_peer(j))

    def adapters(l):
        inv = inv_v[l][:, :RANK]
        scaled = (2.0 * inv * ad_v[l].astype(F32)).astype(BF16)
        la_v[l] = dot(scaled, h_v[l], ((0,), (0,)))
        low = (2.0 * inv * hd_v[l]).astype(BF16)
        part = dot(low, gathered(l, slice(0, TOKENS)), ((0,), (0,)))
        for j in range(TP):
            lbs_v[l, j] = part[:, 128 * j : 128 * j + 128].astype(BF16)
        lbr_v[l, tp] = lbs_v[l, tp]
        for j in range(1, TP):
            lora_b_copy(l, j, lax.rem(tp + j, TP), tp).start()
        pltpu.make_async_copy(la_v.at[l], la_hbm.at[l], out_sem.at[l]).start()

    def adapters_end(l):
        for j in range(1, TP):
            lora_b_copy(l, j, 0, lax.rem(tp - j + TP, TP)).wait_recv()
        total = lbr_v[l, 0].astype(F32)
        for i in range(1, TP):
            total = total + lbr_v[l, i].astype(F32)
        lb_v[l] = total
        pltpu.make_async_copy(lb_v.at[l], lb_hbm.at[l], out_sem.at[LAYERS + l]).start()

    def core_copy(chunk):
        at = index(chunk)
        return remote(
            t_v.at[chunk[0], spans(chunk), 1 - core], tp_v.at[chunk[0], spans(chunk)],
            cs_sem.at[at], cr_sem.at[at], core_peer,
        )

    def to_owner(chunk, j, place):
        at = index(chunk)
        return remote(
            p_v.at[chunk[0], spans(chunk), chip_index(j)], q8_v.at[chunk[0], place, spans(chunk)],
            p1s_sem.at[at, j - 1], p1r_sem.at[at, j - 1], chip_peer(j),
        )

    def from_owner(chunk, j, place):
        at = index(chunk)
        return remote(
            rs_v.at[chunk[0], chip_index(j), spans(chunk)], rr_v.at[chunk[0], spans(chunk), place],
            p2s_sem.at[at, j - 1], p2r_sem.at[at, j - 1], chip_peer(j),
        )

    def source(j):
        return lax.rem(chip - j + CHIPS, CHIPS)

    def pair_sums(chunk):
        l, ts = chunk[0], spans(chunk)
        core_copy(chunk).wait_recv()
        both = t_v[l, ts, core].astype(F32) + tp_v[l, ts].astype(F32)
        p_v[l, ts] = both.reshape(chunk[2], CHIPS, ROWS, WIDTH).astype(BF16)
        for j in (2, 1, 3):
            to_owner(chunk, j, chip).start()
        q8_v[l, chip, ts] = p_v[l, ts, chip]

    def total_copy(chunk):
        at = index(chunk)
        return remote(
            tots_v.at[chunk[0], spans(chunk)], totr_v.at[chunk[0], spans(chunk)],
            hs_sem.at[at], hr_sem.at[at], half_peer,
        )

    def totals(chunk):
        l, ts = chunk[0], spans(chunk)
        for j in range(1, CHIPS):
            to_owner(chunk, j, source(j)).wait_recv()
        total = q8_v[l, 0, ts].astype(F32)
        for i in range(1, CHIPS):
            total = total + q8_v[l, i, ts].astype(F32)
        tots_v[l, ts] = total.astype(BF16)
        total_copy(chunk).start()

    def suffix(chunk):
        l, ts = chunk[0], spans(chunk)
        if l == LAYERS - 1:
            if chunk[1] == 0:
                copies["top"].wait()
            weights = jnp.concatenate([weight_v[ts, core, chip]] * (WIDTH // 128), axis=2)
            carry = weights * top_v[ts].astype(F32)
        else:
            carry = carry_v[ts]
        total_copy(chunk).wait_recv()
        above = totr_v[l, ts].astype(F32)
        carry_v[ts] = carry + above + tots_v[l, ts].astype(F32)
        carry = carry + (1 - half).astype(F32) * above
        for i in reversed(range(CHIPS)):
            rs_v[l, i, ts] = carry.astype(BF16)
            carry = carry + q8_v[l, i, ts].astype(F32)
        for j in (2, 1, 3):
            from_owner(chunk, j, chip).start()
        rr_v[l, ts, chip] = rs_v[l, chip, ts]

    def out_copy(chunk):
        at = index(chunk)
        return remote(
            peer_v.at[chunk[0], spans(chunk)], out_hbm.at[chunk[0], spans(chunk), core],
            os_sem.at[at], or_sem.at[at], core_peer,
        )

    def out_in(chunk):
        at = index(chunk)
        return remote(
            peer_v.at[chunk[0], spans(chunk)], out_hbm.at[chunk[0], spans(chunk), 1 - core],
            os_sem.at[at], or_sem.at[at], core_peer,
        )

    def out_here(chunk):
        return pltpu.make_async_copy(
            own_v.at[chunk[0], spans(chunk)], out_hbm.at[chunk[0], spans(chunk), core], out_sem.at[2 * LAYERS + index(chunk)]
        )

    def finish(chunk):
        l, ts = chunk[0], spans(chunk)
        for j in range(1, CHIPS):
            from_owner(chunk, j, source(j)).wait_recv()
        first = (1 - core).astype(F32)
        second = core.astype(F32)
        carry = rr_v[l, ts].astype(F32).reshape(chunk[2], HALF, WIDTH)
        term = t_v[l, ts, core].astype(F32)
        peer_term = tp_v[l, ts].astype(F32)
        peer_v[l, ts] = (carry + peer_term + second * term).astype(BF16)
        out_copy(chunk).start()
        own_v[l, ts] = (carry + term + first * peer_term).astype(BF16)
        out_here(chunk).start()

    attention(2)
    pl.semaphore_wait(barrier, TP + CHIPS)
    gather_1((2, 0, 1))
    gather_1((2, 1, 1))
    attention(1)
    gather_1((1, 1, 1))
    gather_2((2, 0, 1))
    gather_1((1, 0, 1))
    squares_and_low()
    squares_send()
    gather_2((2, 1, 1))
    gather_2((1, 0, 1))
    gather_3((2, 0, 1))
    gather_4((2, 0, 1))
    gather_3((2, 1, 1))
    attention(0)
    gather_2((1, 1, 1))
    squares_wait()
    gather_4((2, 1, 1))
    gather_4((1, 0, 1))
    gather_3((1, 0, 1))
    gather_end((2, 0, 1))
    products((2, 0, 1))
    gather_4((1, 1, 1))
    gather_3((1, 1, 1))
    gather_1((0, 0, 1))
    gather_end((2, 1, 1))
    products((2, 1, 1))
    gather_1((0, 1, 1))
    gather_end((1, 0, 1))
    products((1, 0, 1))
    terms((2, 0, 1))
    core_copy((2, 0, 1)).start()
    gather_2((0, 0, 1))
    gather_end((1, 1, 1))
    products((1, 1, 1))
    pair_sums((2, 0, 1))
    terms((2, 1, 1))
    gather_3((0, 0, 1))
    core_copy((2, 1, 1)).start()
    gather_2((0, 1, 1))
    adapters(1)
    gather_4((0, 0, 1))
    terms((1, 0, 1))
    pair_sums((2, 1, 1))
    core_copy((1, 0, 1)).start()
    terms((1, 1, 1))
    gather_3((0, 1, 1))
    core_copy((1, 1, 1)).start()
    pair_sums((1, 0, 1))
    gather_4((0, 1, 1))
    totals((2, 0, 1))
    gather_end((0, 0, 1))
    products((0, 0, 1))
    pair_sums((1, 1, 1))
    totals((2, 1, 1))
    gather_end((0, 1, 1))
    suffix((2, 0, 1))
    products((0, 1, 1))
    suffix((2, 1, 1))
    terms((0, 0, 1))
    core_copy((0, 0, 1)).start()
    adapters(2)
    totals((1, 0, 1))
    pair_sums((0, 0, 1))
    adapters(0)
    terms((0, 1, 1))
    core_copy((0, 1, 1)).start()
    totals((1, 1, 1))
    finish((2, 0, 1))
    pair_sums((0, 1, 1))
    suffix((1, 0, 1))
    adapters_end(1)
    suffix((1, 1, 1))
    totals((0, 0, 1))
    adapters_end(0)
    totals((0, 1, 1))
    suffix((0, 0, 1))
    adapters_end(2)
    finish((2, 1, 1))
    suffix((0, 1, 1))
    finish((1, 1, 1))
    finish((1, 0, 1))
    finish((0, 0, 1))
    finish((0, 1, 1))

    for chunk in GATHER_CHUNKS:
        for i in range(7):
            gather_out(chunk, i).wait_send()
    for chunk in PRODUCT_CHUNKS:
        for j in range(1, TP):
            inner_copy(chunk, j, tp).wait_send()
    for chunk in SUM_CHUNKS:
        out_in(chunk).wait_recv()
        out_copy(chunk).wait_send()
        out_here(chunk).wait()
        core_copy(chunk).wait_send()
        total_copy(chunk).wait_send()
        for j in range(1, CHIPS):
            to_owner(chunk, j, chip).wait_send()
            from_owner(chunk, j, chip).wait_send()
    for l in range(LAYERS):
        pltpu.make_async_copy(la_v.at[l], la_hbm.at[l], out_sem.at[l]).wait()
        pltpu.make_async_copy(lb_v.at[l], lb_hbm.at[l], out_sem.at[LAYERS + l]).wait()
        for j in range(1, TP):
            lora_b_copy(l, j, lax.rem(tp + j, TP), tp).wait_send()
    for j in range(1, TP):
        squares_copy(j, tp).wait_send()


def place(grad_ref, a_ref, b_ref, grad_out, a_out, b_out, grad_v, a_v, b_v, in_sem, out_sem):
    pieces = [(a_ref, a_v, a_out), (b_ref, b_v, b_out)]
    for l in range(LAYERS):
        for t in range(2):
            at = (l, t)
            pieces.append((grad_ref.at[at], grad_v.at[at], grad_out.at[at]))
    reads = [pltpu.make_async_copy(src, mid, in_sem.at[i]) for i, (src, mid, _) in enumerate(pieces)]
    writes = [pltpu.make_async_copy(mid, dst, out_sem.at[i]) for i, (_, mid, dst) in enumerate(pieces)]
    for copy in reads:
        copy.start()
    for read, write in zip(reads, writes):
        read.wait()
        write.start()
    for copy in writes:
        copy.wait()


def per_device(
    queries, attention_output_grads, keys, hidden, value_weight, value_down_matrix, value_up_matrix,
    document_index, advantage, loss_token_mask, top_stream_gradient,
):
    hbm = pl.BlockSpec(memory_space=pl.ANY)
    vmem = pl.BlockSpec(memory_space=pltpu.VMEM)
    dma = pltpu.SemaphoreType.DMA
    scratch = [
        pltpu.VMEM((LAYERS, TOKENS, WIDTH), BF16),
        pltpu.VMEM((LAYERS, TOKENS, WIDTH), BF16),
        pltpu.VMEM((LAYERS, TOKENS, HEAD), BF16),
        pltpu.VMEM((LAYERS, TOKENS, WIDTH), BF16),
        pltpu.VMEM((LAYERS, WIDTH, WIDTH), BF16),
        pltpu.VMEM((LAYERS, RANK, WIDTH), BF16),
        pltpu.VMEM((LAYERS, RANK, WIDTH), BF16),
        pltpu.VMEM((2, ROWS, WIDTH), BF16),
        pltpu.VMEM((1152, 128), F32),
        pltpu.VMEM((2, 2, CHIPS, ROWS, 128), F32),
        pltpu.VMEM((TOKENS, 128), F32),
        pltpu.VMEM((LAYERS, TP, TOKENS, HEAD), BF16),
        pltpu.VMEM((LAYERS, TOKENS, RANK), F32),
        pltpu.VMEM((LAYERS, TOKENS, RANK), BF16),
        pltpu.VMEM((2, TOKENS, WIDTH), F32),
        pltpu.VMEM((LAYERS, TOKENS, 128), F32),
        pltpu.VMEM((16, 128), F32),
        pltpu.VMEM((TP, 16, 128), F32),
        pltpu.VMEM((2 * LAYERS, 8, 128), F32),
        pltpu.VMEM((2 * LAYERS, TP, 8, 128), F32),
        pltpu.VMEM((LAYERS, TP, RANK, HEAD), BF16),
        pltpu.VMEM((LAYERS, TP, RANK, HEAD), BF16),
        pltpu.VMEM((LAYERS, RANK, WIDTH), F32),
        pltpu.VMEM((LAYERS, RANK, HEAD), F32),
        pltpu.VMEM((LAYERS, 2, 2, HALF, WIDTH), BF16),
        pltpu.VMEM((LAYERS, 2, HALF, WIDTH), BF16),
        pltpu.VMEM((LAYERS, 2, CHIPS, ROWS, WIDTH), BF16),
        pltpu.VMEM((LAYERS, CHIPS, 2, ROWS, WIDTH), BF16),
        pltpu.VMEM((LAYERS, CHIPS, 2, ROWS, WIDTH), BF16),
        pltpu.VMEM((LAYERS, 2, CHIPS, ROWS, WIDTH), BF16),
        pltpu.VMEM((2, ROWS, WIDTH), F32),
        pltpu.VMEM((LAYERS, 2, ROWS, WIDTH), BF16),
        pltpu.VMEM((LAYERS, 2, ROWS, WIDTH), BF16),
        pltpu.VMEM((LAYERS, 2, HALF, WIDTH), BF16),
        pltpu.VMEM((LAYERS, 2, HALF, WIDTH), BF16),
        dma((16,)), dma((4 * LAYERS,)),
        dma((2 * LAYERS, 7)), dma((2 * LAYERS, 7)), dma((7,)), dma((7,)), dma((2 * LAYERS, 7)), dma((2 * LAYERS, 7)),
        dma((LAYERS, 7)), dma((LAYERS, 7)),
        dma((2 * LAYERS,)), dma((2 * LAYERS,)),
        dma((2 * LAYERS, 7)), dma((2 * LAYERS, 7)), dma((2 * LAYERS, 7)), dma((2 * LAYERS, 7)),
        dma((2 * LAYERS,)), dma((2 * LAYERS,)),
        dma((2 * LAYERS,)), dma((2 * LAYERS,)),
    ]
    grad_in, lora_a, lora_b = pl.pallas_call(
        kernel,
        name="value_backward",
        out_shape=(
            jax.ShapeDtypeStruct((LAYERS, 2, 2, HALF, WIDTH), BF16),
            jax.ShapeDtypeStruct((LAYERS, RANK, WIDTH), F32),
            jax.ShapeDtypeStruct((LAYERS, RANK, HEAD), F32),
        ),
        in_specs=[hbm] * 8 + [vmem] * 3,
        out_specs=(hbm, hbm, hbm),
        scratch_shapes=scratch,
        compiler_params=pltpu.CompilerParams(
            collective_id=0, has_side_effects=True, vmem_limit_bytes=60 << 20
        ),
        cost_estimate=pl.CostEstimate(flops=8_000_000_000, bytes_accessed=22_000_000, transcendentals=4_000_000),
    )(
        queries[0], attention_output_grads[0], keys[0], hidden[0], value_weight[0], jnp.swapaxes(value_down_matrix[0], 1, 2),
        value_up_matrix[0], top_stream_gradient.reshape(2, 2, CHIPS, ROWS, WIDTH),
        document_index.reshape(1, TOKENS), advantage.reshape(1, TOKENS), loss_token_mask.reshape(1, TOKENS),
    )
    grad_in, lora_a, lora_b = pl.pallas_call(
        place,
        name="place",
        out_shape=(
            jax.ShapeDtypeStruct(grad_in.shape, BF16),
            jax.ShapeDtypeStruct(lora_a.shape, F32),
            jax.ShapeDtypeStruct(lora_b.shape, F32),
        ),
        in_specs=[hbm] * 3,
        out_specs=(hbm, hbm, hbm),
        scratch_shapes=[
            pltpu.VMEM(grad_in.shape, BF16),
            pltpu.VMEM(lora_a.shape, F32),
            pltpu.VMEM(lora_b.shape, F32),
            dma((8,)), dma((8,)),
        ],
        compiler_params=pltpu.CompilerParams(vmem_limit_bytes=60 << 20),
    )(grad_in, lora_a, lora_b)
    return grad_in.reshape(1, LAYERS, TOKENS, WIDTH), jnp.swapaxes(lora_a, 1, 2)[None], lora_b[None]


def solution(mesh):
    in_specs = (
        P("pp", None, None, "tp"),
        P("pp", None, None, "tp"),
        P("pp", None, None, "tp"),
        P("pp", None, None, "tp"),
        P("pp", None, "tp", None),
        P("pp", None, "tp", None),
        P("pp", None, None, None),
        P(),
        P(),
        P(),
        P(None, "tp"),
    )
    out_specs = (P("pp", None, None, "tp"), P("pp", None, "tp", None), P("pp", None, None, "tp"))
    return jax.shard_map(
        per_device, mesh=mesh, in_specs=in_specs, out_specs=out_specs, check_vma=False
    )
```

```python
import jax
import jax.numpy as jnp
from jax import lax
from jax.experimental import pallas as pl
from jax.experimental.pallas import tpu as pltpu
from jax.sharding import PartitionSpec as P

MESH = pl.DeviceIdType.MESH
BF16 = jnp.bfloat16
F32 = jnp.float32
LAYERS = 3
TOKENS = 512
WIDTH = 1024
HEAD = 128
HEADS = 8
RANK = 64
SPAN = 256
HALF = 128
ROWS = 32
CHIPS = 4
TP = 8
MODEL = 8192
SEGS = 8
LOG2E = 1.4426950408889634
ALONG_CHUNKS = ((2, 0, 1), (1, 1, 1), (0, 1, 1), )
GATHER_CHUNKS = ((2, 1, 1), (1, 0, 1), (0, 0, 1))
PRODUCT_CHUNKS = ((2, 0, 1), (2, 1, 1), (1, 0, 1), (1, 1, 1), (0, 0, 1), (0, 1, 1))
SUM_CHUNKS = ((2, 0, 1), (2, 1, 1), (1, 0, 1), (0, 0, 1), (1, 1, 1), (0, 1, 1))
SOFTMAX_SCALE = HEAD**-0.5 * LOG2E
MASK_OFFSET = (0, 128, 384, 768)


def dot(a, b, dims):
    return lax.dot_general(a, b, (dims, ((), ())), preferred_element_type=F32)


def kernel(
    q_hbm, g_hbm, k_hbm, h_hbm, w_hbm, dn_hbm, up_hbm, top_hbm, doc_ref, adv_ref, loss_ref,
    out_hbm, la_hbm, lb_hbm,
    q_v, g_v, k_v, h_v, w_v, dn_v, up_v, top_v,
    mask_v, weight_v, acc_v, vg_v, hd_v, ad_v, ng_v, inv_v,
    sqs_v, sqr_v, ins_v, inr_v, lbs_v, lbr_v, la_v, lb_v,
    t_v, tp_v, p_v, q8_v, rs_v, rr_v, carry_v, tots_v, totr_v, own_v, peer_v,
    in_sem, out_sem,
    gs_sem, gr_sem, sqs_sem, sqr_sem, ins_sem, inr_sem, lbs_sem, lbr_sem,
    cs_sem, cr_sem, p1s_sem, p1r_sem, p2s_sem, p2r_sem, hs_sem, hr_sem, os_sem, or_sem,
):
    pp = lax.axis_index("pp")
    tp = lax.axis_index("tp")
    core = lax.rem(pp, 2)
    chip = lax.rem(lax.div(pp, 2), CHIPS)
    half = lax.div(pp, 2 * CHIPS)
    yl = lax.div(tp, 4)
    x = lax.rem(tp, 4)

    yl_peer = (pp, (1 - yl) * 4 + x)
    x_up = (pp, yl * 4 + lax.rem(x + 1, 4))
    x_down = (pp, yl * 4 + lax.rem(x + 3, 4))
    core_peer = (pp + 1 - 2 * core, tp)
    half_peer = (lax.rem(pp + 2 * CHIPS, 4 * CHIPS), tp)

    def tp_peer(j):
        return (pp, lax.rem(tp + j, TP))

    def chip_index(j):
        return lax.rem(chip + j, CHIPS)

    def chip_peer(j):
        return ((half * CHIPS + chip_index(j)) * 2 + core, tp)

    copies = {}

    def load(name, src, dst):
        copies[name] = pltpu.make_async_copy(src, dst, in_sem.at[len(copies)])

    for l in (2, 1, 0):
        load(("k", l), k_hbm.at[l], k_v.at[l])
        load(("q", l), q_hbm.at[l], q_v.at[l])
        load(("g", l), g_hbm.at[l], g_v.at[l])
    load("h", h_hbm, h_v)
    load("dn", dn_hbm, dn_v)
    load("up", up_hbm, up_v)
    for l in (2, 1, 0):
        load(("w", l), w_hbm.at[l], w_v.at[l])
    load("top", top_hbm.at[:, core, chip], top_v)
    first = [(name, LAYERS - 1) for name in "kqg"]
    for name in first:
        copies[name].start()

    barrier = pltpu.get_barrier_semaphore()
    for j in range(1, TP):
        pl.semaphore_signal(barrier, inc=1, device_id=tp_peer(j), device_id_type=MESH)
    for j in range(1, CHIPS):
        pl.semaphore_signal(barrier, inc=1, device_id=chip_peer(j), device_id_type=MESH)
    for peer in (core_peer, half_peer):
        pl.semaphore_signal(barrier, inc=1, device_id=peer, device_id_type=MESH)

    def remote(src, dst, send, recv, device):
        return pltpu.make_async_remote_copy(
            src_ref=src, dst_ref=dst, send_sem=send, recv_sem=recv, device_id=device, device_id_type=MESH
        )

    def columns(row):
        return jnp.transpose(jnp.broadcast_to(row, (128, TOKENS)))

    def rows_of(sums):
        parts = [sums[128 * i : 128 * i + 128, :] for i in range(sums.shape[0] // 128)]
        return jnp.concatenate([jnp.sum(jnp.transpose(part), axis=0, keepdims=True) for part in parts], axis=0)

    def columns_of(rows):
        return jnp.concatenate(
            [jnp.transpose(jnp.broadcast_to(rows[i : i + 1, :], (128, 128))) for i in range(rows.shape[0])], axis=0
        )

    doc_row = doc_ref[...].astype(F32)
    doc_col = columns(doc_row)
    key_pos = lax.broadcasted_iota(jnp.int32, (128, 128), 0)
    query_pos = lax.broadcasted_iota(jnp.int32, (128, 128), 1)
    for b in range(4):
        low = max(0, b - 2)
        for kb in range(low, b + 1):
            allowed = doc_col[128 * kb : 128 * kb + 128, :] == doc_row[:, 128 * b : 128 * b + 128]
            if kb == b:
                allowed = allowed & (key_pos <= query_pos)
            at = MASK_OFFSET[b] + 128 * (kb - low)
            mask_v[at : at + 128, :] = jnp.where(allowed, 0.0, -jnp.inf)
    loss_row = loss_ref[...].astype(F32)
    labels = lax.broadcasted_iota(jnp.int32, (SEGS, TOKENS), 0).astype(F32)
    member = jnp.where(labels == doc_row, 1.0, 0.0)
    counts = jnp.sum(member * loss_row, axis=1, keepdims=True)
    per_token = jnp.sum(member * (1.0 / jnp.maximum(counts, 1.0)), axis=0, keepdims=True)
    weights = columns(adv_ref[...].astype(F32) * loss_row * per_token * (TOKENS / SEGS))
    weight_v[...] = weights.reshape(2, 2, CHIPS, ROWS, 128)

    slot = x * 2 + yl
    other = x * 2 + (1 - yl)
    left = lax.rem(x + 3, 4) * 2
    right = lax.rem(x + 1, 4) * 2
    across = lax.rem(x + 2, 4) * 2

    def attention(l):
        for name in ("k", "q", "g"):
            copies[(name, l)].wait()
        if l == LAYERS - 1:
            for name in copies:
                if name not in first:
                    copies[name].start()
        for b in range(4):
            low, high = max(0, b - 2) * 128, (b + 1) * 128
            keys = k_v[l, low:high, :]
            mask = mask_v[MASK_OFFSET[b] : MASK_OFFSET[b] + high - low, :]
            mask4 = jnp.concatenate([mask] * 4, axis=1)
            total = None
            for part in range(2):
                heads = range(4 * part, 4 * part + 4)
                block = slice(128 * b, 128 * b + 128)
                queries = jnp.concatenate([q_v[l, block, HEAD * i : HEAD * i + HEAD] for i in heads], axis=0)
                grads = jnp.concatenate([g_v[l, block, HEAD * i : HEAD * i + HEAD] for i in heads], axis=0)
                scores = dot(keys, queries, ((1,), (1,))) + mask4
                peak = jnp.max(scores, axis=0, keepdims=True)
                expo = jnp.exp2((scores - peak) * SOFTMAX_SCALE)
                probs = (expo * (1.0 / jnp.sum(expo, axis=0, keepdims=True))).astype(BF16)
                piece = dot(probs, grads, ((1,), (0,)))
                total = piece if total is None else total + piece
            if b == 0:
                acc_v[0:128, :] = total
            else:
                acc_v[low : high - 128, :] += total[: high - low - 128]
                acc_v[high - 128 : high, :] = total[high - low - 128 :]
        vg_v[l, slot] = acc_v[...].astype(BF16)

    def spans(chunk):
        return pl.ds(chunk[1], chunk[2])

    def tokens(chunk):
        return slice(chunk[1] * SPAN, (chunk[1] + chunk[2]) * SPAN)

    def index(chunk):
        return chunk[0] * 2 + chunk[1]

    def gather_copy(chunk, i, place, device):
        part = vg_v.at[chunk[0], place, pl.ds(chunk[1] * SPAN, chunk[2] * SPAN)]
        return remote(part, part, gs_sem.at[index(chunk), i], gr_sem.at[index(chunk), i], device)

    def gather_out(chunk, i):
        return (
            lambda: gather_copy(chunk, 0, slot, yl_peer),
            lambda: gather_copy(chunk, 1, slot, x_up),
            lambda: gather_copy(chunk, 2, slot, x_down),
            lambda: gather_copy(chunk, 3, other, x_up),
            lambda: gather_copy(chunk, 4, other, x_down),
            lambda: gather_copy(chunk, 5, left + yl, x_up),
            lambda: gather_copy(chunk, 6, right + (1 - yl), x_down),
        )[i]()

    def gather_in(chunk, i):
        place = (other, left + yl, right + yl, left + (1 - yl), right + (1 - yl), across + yl, across + (1 - yl))[i]
        return gather_copy(chunk, i, place, yl_peer)

    def gather_1(chunk):
        for i in (0, 1, 2):
            gather_out(chunk, i).start()

    def gather_2(chunk):
        gather_in(chunk, 0).wait_recv()
        for i in (3, 4):
            gather_out(chunk, i).start()

    def gather_3(chunk):
        gather_in(chunk, 1).wait_recv()
        gather_out(chunk, 5).start()

    def gather_4(chunk):
        gather_in(chunk, 4).wait_recv()
        gather_out(chunk, 6).start()

    def gather_end(chunk):
        for i in (2, 3, 5, 6):
            gather_in(chunk, i).wait_recv()

    def along_copy(chunk, i, place, device, first=0, count=SPAN):
        part = vg_v.at[chunk[0], place, pl.ds(chunk[1] * SPAN + first, count)]
        return remote(part, part, gs_sem.at[index(chunk), i], gr_sem.at[index(chunk), i], device)

    def along_out(chunk, i):
        return (
            lambda: along_copy(chunk, 0, slot, yl_peer),
            lambda: along_copy(chunk, 1, slot, x_up),
            lambda: along_copy(chunk, 2, slot, x_down),
            lambda: along_copy(chunk, 3, left + yl, yl_peer),
            lambda: along_copy(chunk, 4, right + yl, yl_peer),
            lambda: along_copy(chunk, 5, left + yl, x_up, 0, HALF),
            lambda: along_copy(chunk, 6, right + yl, x_down, HALF, HALF),
            lambda: along_copy(chunk, 7, across + yl, yl_peer),
        )[i]()

    def along_in(chunk, i):
        return (
            lambda: along_copy(chunk, 0, other, yl_peer),
            lambda: along_copy(chunk, 1, left + yl, x_up),
            lambda: along_copy(chunk, 2, right + yl, x_down),
            lambda: along_copy(chunk, 3, left + (1 - yl), yl_peer),
            lambda: along_copy(chunk, 4, right + (1 - yl), yl_peer),
            lambda: along_copy(chunk, 5, across + yl, x_up, 0, HALF),
            lambda: along_copy(chunk, 6, across + yl, x_down, HALF, HALF),
            lambda: along_copy(chunk, 7, across + (1 - yl), yl_peer),
        )[i]()

    def along_1(chunk):
        for i in (1, 2, 0):
            along_out(chunk, i).start()

    def along_2(chunk):
        along_in(chunk, 1).wait_recv()
        along_in(chunk, 2).wait_recv()
        for i in (5, 6, 3, 4):
            along_out(chunk, i).start()

    def along_3(chunk):
        along_in(chunk, 5).wait_recv()
        along_in(chunk, 6).wait_recv()
        along_out(chunk, 7).start()

    def along_end(chunk):
        for i in (0, 3, 4, 7):
            along_in(chunk, i).wait_recv()

    def squares_and_low():
        sqs_v[...] = jnp.zeros((16, 128), F32)
        copies["h"].wait()
        copies["dn"].wait()
        for l in range(LAYERS):
            sums = None
            for n in range(WIDTH // 128):
                part = h_v[l, :, 128 * n : 128 * n + 128].astype(F32)
                sums = part * part if sums is None else sums + part * part
            sqs_v[4 * l : 4 * l + 4, :] = rows_of(sums)
            hd_v[l] = dot(h_v[l], dn_v[l], ((1,), (1,)))
        sqr_v[tp] = sqs_v[...]

    def squares_copy(j, place):
        return remote(sqs_v, sqr_v.at[place], sqs_sem.at[j - 1], sqr_sem.at[j - 1], tp_peer(j))

    def squares_send():
        for j in range(1, TP):
            squares_copy(j, tp).start()

    def squares_wait():
        for j in range(1, TP):
            squares_copy(j, lax.rem(tp - j + TP, TP)).wait_recv()
        total = sqr_v[0]
        for i in range(1, TP):
            total = total + sqr_v[i]
        inverse = lax.rsqrt(total * (1.0 / MODEL) + 1e-5)
        for l in range(LAYERS):
            inv_v[l] = columns_of(inverse[4 * l : 4 * l + 4, :])

    def gathered(l, rows):
        return jnp.concatenate([vg_v[l, (j % 4) * 2 + j // 4, rows] for j in range(TP)], axis=1)

    def inner_copy(chunk, j, place):
        at = index(chunk)
        return remote(ins_v.at[at], inr_v.at[at, place], ins_sem.at[at, j - 1], inr_sem.at[at, j - 1], tp_peer(j))

    def products(chunk):
        l, at, rows = chunk[0], index(chunk), tokens(chunk)
        if l == LAYERS - 1 and chunk[1] == 0:
            copies["up"].wait()
        if chunk[1] == 0:
            copies[("w", l)].wait()
        ad_v[l, rows] = dot(gathered(l, rows), up_v[l], ((1,), (1,))).astype(BF16)
        acc_v[rows] = jnp.zeros((chunk[2] * SPAN, 128), F32)

        def one(n, unused):
            cols = pl.ds(pl.multiple_of(n * 256, 256), 256)
            twice = (ad_v[l, rows].astype(F32) * 2.0).astype(BF16)
            ng = dot(gathered(l, rows), w_v[l, cols, :], ((1,), (1,))) + dot(twice, dn_v[l, :, cols], ((1,), (0,)))
            ng_v[l % 2, rows, cols] = ng
            prod = h_v[l, rows, cols].astype(F32) * ng
            acc_v[rows] += prod[:, :128] + prod[:, 128:]
            return unused

        lax.fori_loop(0, WIDTH // 256, one, 0)
        row = rows_of(acc_v[rows])
        ins_v[at] = jnp.concatenate([row] * (4 // chunk[2]), axis=0)
        inr_v[at, tp] = ins_v[at]
        for j in range(1, TP):
            inner_copy(chunk, j, tp).start()

    def terms(chunk):
        l, at, rows = chunk[0], index(chunk), tokens(chunk)
        for j in range(1, TP):
            inner_copy(chunk, j, lax.rem(tp - j + TP, TP)).wait_recv()
        total = inr_v[at, 0]
        for i in range(1, TP):
            total = total + inr_v[at, i]
        inv = inv_v[l, rows]
        acc_v[rows] = inv * inv * inv * columns_of(total[0 : 2 * chunk[2], :]) * (1.0 / MODEL)

        def one(n, unused):
            cols = pl.ds(pl.multiple_of(n * 128, 128), 128)
            term = inv_v[l, rows] * ng_v[l % 2, rows, cols] - acc_v[rows] * h_v[l, rows, cols].astype(F32)
            t_v[l, spans(chunk), :, :, cols] = term.astype(BF16).reshape(chunk[2], 2, HALF, 128)
            return unused

        lax.fori_loop(0, WIDTH // 128, one, 0)

    def lora_b_copy(l, j, block, place):
        return remote(lbs_v.at[l, block], lbr_v.at[l, place], lbs_sem.at[l, j - 1], lbr_sem.at[l, j - 1], tp_peer(j))

    def adapters(l):
        inv = inv_v[l][:, :RANK]
        scaled = (2.0 * inv * ad_v[l].astype(F32)).astype(BF16)
        la_v[l] = dot(scaled, h_v[l], ((0,), (0,)))
        low = (2.0 * inv * hd_v[l]).astype(BF16)
        part = dot(low, gathered(l, slice(0, TOKENS)), ((0,), (0,)))
        for j in range(TP):
            lbs_v[l, j] = part[:, 128 * j : 128 * j + 128].astype(BF16)
        lbr_v[l, tp] = lbs_v[l, tp]
        for j in range(1, TP):
            lora_b_copy(l, j, lax.rem(tp + j, TP), tp).start()
        pltpu.make_async_copy(la_v.at[l], la_hbm.at[l], out_sem.at[l]).start()

    def adapters_end(l):
        for j in range(1, TP):
            lora_b_copy(l, j, 0, lax.rem(tp - j + TP, TP)).wait_recv()
        total = lbr_v[l, 0].astype(F32)
        for i in range(1, TP):
            total = total + lbr_v[l, i].astype(F32)
        lb_v[l] = total
        pltpu.make_async_copy(lb_v.at[l], lb_hbm.at[l], out_sem.at[LAYERS + l]).start()

    def core_copy(chunk):
        at = index(chunk)
        return remote(
            t_v.at[chunk[0], spans(chunk), 1 - core], tp_v.at[chunk[0], spans(chunk)],
            cs_sem.at[at], cr_sem.at[at], core_peer,
        )

    def to_owner(chunk, j, place):
        at = index(chunk)
        return remote(
            p_v.at[chunk[0], spans(chunk), chip_index(j)], q8_v.at[chunk[0], place, spans(chunk)],
            p1s_sem.at[at, j - 1], p1r_sem.at[at, j - 1], chip_peer(j),
        )

    def from_owner(chunk, j, place):
        at = index(chunk)
        return remote(
            rs_v.at[chunk[0], chip_index(j), spans(chunk)], rr_v.at[chunk[0], spans(chunk), place],
            p2s_sem.at[at, j - 1], p2r_sem.at[at, j - 1], chip_peer(j),
        )

    def source(j):
        return lax.rem(chip - j + CHIPS, CHIPS)

    def pair_sums(chunk):
        l, ts = chunk[0], spans(chunk)
        core_copy(chunk).wait_recv()
        both = t_v[l, ts, core].astype(F32) + tp_v[l, ts].astype(F32)
        p_v[l, ts] = both.reshape(chunk[2], CHIPS, ROWS, WIDTH).astype(BF16)
        for j in (2, 1, 3):
            to_owner(chunk, j, chip).start()
        q8_v[l, chip, ts] = p_v[l, ts, chip]

    def total_copy(chunk):
        at = index(chunk)
        return remote(
            tots_v.at[chunk[0], spans(chunk)], totr_v.at[chunk[0], spans(chunk)],
            hs_sem.at[at], hr_sem.at[at], half_peer,
        )

    def totals(chunk):
        l, ts = chunk[0], spans(chunk)
        for j in range(1, CHIPS):
            to_owner(chunk, j, source(j)).wait_recv()
        total = q8_v[l, 0, ts].astype(F32)
        for i in range(1, CHIPS):
            total = total + q8_v[l, i, ts].astype(F32)
        tots_v[l, ts] = total.astype(BF16)
        total_copy(chunk).start()

    def suffix(chunk):
        l, ts = chunk[0], spans(chunk)
        if l == LAYERS - 1:
            if chunk[1] == 0:
                copies["top"].wait()
            weights = jnp.concatenate([weight_v[ts, core, chip]] * (WIDTH // 128), axis=2)
            carry = weights * top_v[ts].astype(F32)
        else:
            carry = carry_v[ts]
        total_copy(chunk).wait_recv()
        above = totr_v[l, ts].astype(F32)
        carry_v[ts] = carry + above + tots_v[l, ts].astype(F32)
        carry = carry + (1 - half).astype(F32) * above
        for i in reversed(range(CHIPS)):
            rs_v[l, i, ts] = carry.astype(BF16)
            carry = carry + q8_v[l, i, ts].astype(F32)
        for j in (2, 1, 3):
            from_owner(chunk, j, chip).start()
        rr_v[l, ts, chip] = rs_v[l, chip, ts]

    def out_copy(chunk):
        at = index(chunk)
        return remote(
            peer_v.at[chunk[0], spans(chunk)], out_hbm.at[chunk[0], spans(chunk), core],
            os_sem.at[at], or_sem.at[at], core_peer,
        )

    def out_in(chunk):
        at = index(chunk)
        return remote(
            peer_v.at[chunk[0], spans(chunk)], out_hbm.at[chunk[0], spans(chunk), 1 - core],
            os_sem.at[at], or_sem.at[at], core_peer,
        )

    def out_here(chunk):
        return pltpu.make_async_copy(
            own_v.at[chunk[0], spans(chunk)], out_hbm.at[chunk[0], spans(chunk), core], out_sem.at[2 * LAYERS + index(chunk)]
        )

    def finish(chunk):
        l, ts = chunk[0], spans(chunk)
        for j in range(1, CHIPS):
            from_owner(chunk, j, source(j)).wait_recv()
        first = (1 - core).astype(F32)
        second = core.astype(F32)
        carry = rr_v[l, ts].astype(F32).reshape(chunk[2], HALF, WIDTH)
        term = t_v[l, ts, core].astype(F32)
        peer_term = tp_v[l, ts].astype(F32)
        peer_v[l, ts] = (carry + peer_term + second * term).astype(BF16)
        out_copy(chunk).start()
        own_v[l, ts] = (carry + term + first * peer_term).astype(BF16)
        out_here(chunk).start()

    attention(2)
    pl.semaphore_wait(barrier, TP + CHIPS)
    along_1((2, 0, 1))
    gather_1((2, 1, 1))
    attention(1)
    gather_1((1, 0, 1))
    along_1((1, 1, 1))
    squares_and_low()
    squares_send()
    along_2((2, 0, 1))
    gather_2((2, 1, 1))
    gather_2((1, 0, 1))
    along_3((2, 0, 1))
    along_2((1, 1, 1))
    attention(0)
    gather_3((2, 1, 1))
    gather_4((2, 1, 1))
    squares_wait()
    gather_4((1, 0, 1))
    along_3((1, 1, 1))
    gather_3((1, 0, 1))
    along_end((2, 0, 1))
    products((2, 0, 1))
    gather_1((0, 0, 1))
    along_1((0, 1, 1))
    gather_end((2, 1, 1))
    products((2, 1, 1))
    gather_end((1, 0, 1))
    products((1, 0, 1))
    gather_2((0, 0, 1))
    gather_3((0, 0, 1))
    along_end((1, 1, 1))
    terms((2, 0, 1))
    core_copy((2, 0, 1)).start()
    products((1, 1, 1))
    pair_sums((2, 0, 1))
    terms((2, 1, 1))
    core_copy((2, 1, 1)).start()
    along_2((0, 1, 1))
    gather_4((0, 0, 1))
    terms((1, 0, 1))
    core_copy((1, 0, 1)).start()
    pair_sums((2, 1, 1))
    adapters(2)
    pair_sums((1, 0, 1))
    along_3((0, 1, 1))
    terms((1, 1, 1))
    core_copy((1, 1, 1)).start()
    gather_end((0, 0, 1))
    totals((2, 0, 1))
    products((0, 0, 1))
    pair_sums((1, 1, 1))
    totals((2, 1, 1))
    along_end((0, 1, 1))
    products((0, 1, 1))
    suffix((2, 0, 1))
    terms((0, 0, 1))
    totals((1, 0, 1))
    suffix((2, 1, 1))
    core_copy((0, 0, 1)).start()
    totals((1, 1, 1))
    terms((0, 1, 1))
    pair_sums((0, 0, 1))
    core_copy((0, 1, 1)).start()
    pair_sums((0, 1, 1))
    suffix((1, 0, 1))
    adapters_end(2)
    adapters(1)
    adapters(0)
    finish((2, 0, 1))
    totals((0, 0, 1))
    suffix((1, 1, 1))
    finish((2, 1, 1))
    totals((0, 1, 1))
    suffix((0, 0, 1))
    suffix((0, 1, 1))
    finish((1, 0, 1))
    finish((0, 0, 1))
    adapters_end(1)
    adapters_end(0)
    finish((1, 1, 1))
    finish((0, 1, 1))

    for chunk in GATHER_CHUNKS:
        for i in range(7):
            gather_out(chunk, i).wait_send()
    for chunk in ALONG_CHUNKS:
        for i in range(8):
            along_out(chunk, i).wait_send()
    for chunk in PRODUCT_CHUNKS:
        for j in range(1, TP):
            inner_copy(chunk, j, tp).wait_send()
    for chunk in SUM_CHUNKS:
        out_in(chunk).wait_recv()
        out_copy(chunk).wait_send()
        out_here(chunk).wait()
        core_copy(chunk).wait_send()
        total_copy(chunk).wait_send()
        for j in range(1, CHIPS):
            to_owner(chunk, j, chip).wait_send()
            from_owner(chunk, j, chip).wait_send()
    for l in range(LAYERS):
        pltpu.make_async_copy(la_v.at[l], la_hbm.at[l], out_sem.at[l]).wait()
        pltpu.make_async_copy(lb_v.at[l], lb_hbm.at[l], out_sem.at[LAYERS + l]).wait()
        for j in range(1, TP):
            lora_b_copy(l, j, lax.rem(tp + j, TP), tp).wait_send()
    for j in range(1, TP):
        squares_copy(j, tp).wait_send()


def place(grad_ref, a_ref, b_ref, grad_out, a_out, b_out, grad_v, a_v, b_v, in_sem, out_sem):
    pieces = [(a_ref, a_v, a_out), (b_ref, b_v, b_out)]
    for l in range(LAYERS):
        for t in range(2):
            at = (l, t)
            pieces.append((grad_ref.at[at], grad_v.at[at], grad_out.at[at]))
    reads = [pltpu.make_async_copy(src, mid, in_sem.at[i]) for i, (src, mid, _) in enumerate(pieces)]
    writes = [pltpu.make_async_copy(mid, dst, out_sem.at[i]) for i, (_, mid, dst) in enumerate(pieces)]
    for copy in reads:
        copy.start()
    for read, write in zip(reads, writes):
        read.wait()
        write.start()
    for copy in writes:
        copy.wait()


def per_device(
    queries, attention_output_grads, keys, hidden, value_weight, value_down_matrix, value_up_matrix,
    document_index, advantage, loss_token_mask, top_stream_gradient,
):
    hbm = pl.BlockSpec(memory_space=pl.ANY)
    vmem = pl.BlockSpec(memory_space=pltpu.VMEM)
    dma = pltpu.SemaphoreType.DMA
    scratch = [
        pltpu.VMEM((LAYERS, TOKENS, WIDTH), BF16),
        pltpu.VMEM((LAYERS, TOKENS, WIDTH), BF16),
        pltpu.VMEM((LAYERS, TOKENS, HEAD), BF16),
        pltpu.VMEM((LAYERS, TOKENS, WIDTH), BF16),
        pltpu.VMEM((LAYERS, WIDTH, WIDTH), BF16),
        pltpu.VMEM((LAYERS, RANK, WIDTH), BF16),
        pltpu.VMEM((LAYERS, RANK, WIDTH), BF16),
        pltpu.VMEM((2, ROWS, WIDTH), BF16),
        pltpu.VMEM((1152, 128), F32),
        pltpu.VMEM((2, 2, CHIPS, ROWS, 128), F32),
        pltpu.VMEM((TOKENS, 128), F32),
        pltpu.VMEM((LAYERS, TP, TOKENS, HEAD), BF16),
        pltpu.VMEM((LAYERS, TOKENS, RANK), F32),
        pltpu.VMEM((LAYERS, TOKENS, RANK), BF16),
        pltpu.VMEM((2, TOKENS, WIDTH), F32),
        pltpu.VMEM((LAYERS, TOKENS, 128), F32),
        pltpu.VMEM((16, 128), F32),
        pltpu.VMEM((TP, 16, 128), F32),
        pltpu.VMEM((2 * LAYERS, 8, 128), F32),
        pltpu.VMEM((2 * LAYERS, TP, 8, 128), F32),
        pltpu.VMEM((LAYERS, TP, RANK, HEAD), BF16),
        pltpu.VMEM((LAYERS, TP, RANK, HEAD), BF16),
        pltpu.VMEM((LAYERS, RANK, WIDTH), F32),
        pltpu.VMEM((LAYERS, RANK, HEAD), F32),
        pltpu.VMEM((LAYERS, 2, 2, HALF, WIDTH), BF16),
        pltpu.VMEM((LAYERS, 2, HALF, WIDTH), BF16),
        pltpu.VMEM((LAYERS, 2, CHIPS, ROWS, WIDTH), BF16),
        pltpu.VMEM((LAYERS, CHIPS, 2, ROWS, WIDTH), BF16),
        pltpu.VMEM((LAYERS, CHIPS, 2, ROWS, WIDTH), BF16),
        pltpu.VMEM((LAYERS, 2, CHIPS, ROWS, WIDTH), BF16),
        pltpu.VMEM((2, ROWS, WIDTH), F32),
        pltpu.VMEM((LAYERS, 2, ROWS, WIDTH), BF16),
        pltpu.VMEM((LAYERS, 2, ROWS, WIDTH), BF16),
        pltpu.VMEM((LAYERS, 2, HALF, WIDTH), BF16),
        pltpu.VMEM((LAYERS, 2, HALF, WIDTH), BF16),
        dma((16,)), dma((4 * LAYERS,)),
        dma((2 * LAYERS, 8)), dma((2 * LAYERS, 8)), dma((7,)), dma((7,)), dma((2 * LAYERS, 7)), dma((2 * LAYERS, 7)),
        dma((LAYERS, 7)), dma((LAYERS, 7)),
        dma((2 * LAYERS,)), dma((2 * LAYERS,)),
        dma((2 * LAYERS, 7)), dma((2 * LAYERS, 7)), dma((2 * LAYERS, 7)), dma((2 * LAYERS, 7)),
        dma((2 * LAYERS,)), dma((2 * LAYERS,)),
        dma((2 * LAYERS,)), dma((2 * LAYERS,)),
    ]
    grad_in, lora_a, lora_b = pl.pallas_call(
        kernel,
        name="value_backward",
        out_shape=(
            jax.ShapeDtypeStruct((LAYERS, 2, 2, HALF, WIDTH), BF16),
            jax.ShapeDtypeStruct((LAYERS, RANK, WIDTH), F32),
            jax.ShapeDtypeStruct((LAYERS, RANK, HEAD), F32),
        ),
        in_specs=[hbm] * 8 + [vmem] * 3,
        out_specs=(hbm, hbm, hbm),
        scratch_shapes=scratch,
        compiler_params=pltpu.CompilerParams(
            collective_id=0, has_side_effects=True, vmem_limit_bytes=60 << 20
        ),
        cost_estimate=pl.CostEstimate(flops=8_000_000_000, bytes_accessed=22_000_000, transcendentals=4_000_000),
    )(
        queries[0], attention_output_grads[0], keys[0], hidden[0], value_weight[0], jnp.swapaxes(value_down_matrix[0], 1, 2),
        value_up_matrix[0], top_stream_gradient.reshape(2, 2, CHIPS, ROWS, WIDTH),
        document_index.reshape(1, TOKENS), advantage.reshape(1, TOKENS), loss_token_mask.reshape(1, TOKENS),
    )
    grad_in, lora_a, lora_b = pl.pallas_call(
        place,
        name="place",
        out_shape=(
            jax.ShapeDtypeStruct(grad_in.shape, BF16),
            jax.ShapeDtypeStruct(lora_a.shape, F32),
            jax.ShapeDtypeStruct(lora_b.shape, F32),
        ),
        in_specs=[hbm] * 3,
        out_specs=(hbm, hbm, hbm),
        scratch_shapes=[
            pltpu.VMEM(grad_in.shape, BF16),
            pltpu.VMEM(lora_a.shape, F32),
            pltpu.VMEM(lora_b.shape, F32),
            dma((8,)), dma((8,)),
        ],
        compiler_params=pltpu.CompilerParams(vmem_limit_bytes=60 << 20),
    )(grad_in, lora_a, lora_b)
    return grad_in.reshape(1, LAYERS, TOKENS, WIDTH), jnp.swapaxes(lora_a, 1, 2)[None], lora_b[None]


def solution(mesh):
    in_specs = (
        P("pp", None, None, "tp"),
        P("pp", None, None, "tp"),
        P("pp", None, None, "tp"),
        P("pp", None, None, "tp"),
        P("pp", None, "tp", None),
        P("pp", None, "tp", None),
        P("pp", None, None, None),
        P(),
        P(),
        P(),
        P(None, "tp"),
    )
    out_specs = (P("pp", None, None, "tp"), P("pp", None, "tp", None), P("pp", None, None, "tp"))
    return jax.shard_map(
        per_device, mesh=mesh, in_specs=in_specs, out_specs=out_specs, check_vma=False
    )
```

```python
import jax
import jax.numpy as jnp
from jax import lax
from jax.experimental import pallas as pl
from jax.experimental.pallas import tpu as pltpu
from jax.sharding import PartitionSpec as P

MESH = pl.DeviceIdType.MESH
BF16 = jnp.bfloat16
F32 = jnp.float32
LAYERS = 3
TOKENS = 512
WIDTH = 1024
HEAD = 128
HEADS = 8
RANK = 64
SPAN = 256
HALF = 128
ROWS = 32
CHIPS = 4
TP = 8
MODEL = 8192
SEGS = 8
LOG2E = 1.4426950408889634
ALONG_CHUNKS = ((2, 0, 1), (1, 1, 1), (0, 1, 1), )
GATHER_CHUNKS = ((2, 1, 1), (1, 0, 1), (0, 0, 1))
PRODUCT_CHUNKS = ((2, 0, 1), (2, 1, 1), (1, 0, 1), (1, 1, 1), (0, 0, 1), (0, 1, 1))
SUM_CHUNKS = ((2, 0, 1), (2, 1, 1), (1, 0, 1), (0, 0, 1), (1, 1, 1), (0, 1, 1))
SOFTMAX_SCALE = HEAD**-0.5 * LOG2E
MASK_OFFSET = (0, 128, 384, 768)


def dot(a, b, dims):
    return lax.dot_general(a, b, (dims, ((), ())), preferred_element_type=F32)


def kernel(
    q_hbm, g_hbm, k_hbm, h_hbm, w_hbm, dn_hbm, up_hbm, top_hbm, doc_ref, adv_ref, loss_ref,
    out_hbm, la_hbm, lb_hbm,
    q_v, g_v, k_v, h_v, w_v, dn_v, up_v, top_v,
    mask_v, weight_v, acc_v, vg_v, hd_v, ad_v, ng_v, inv_v,
    sqs_v, sqr_v, ins_v, inr_v, lbs_v, lbr_v, la_v, lb_v,
    t_v, tp_v, p_v, q8_v, rs_v, rr_v, carry_v, tots_v, totr_v, own_v, peer_v,
    in_sem, out_sem,
    gs_sem, gr_sem, sqs_sem, sqr_sem, ins_sem, inr_sem, lbs_sem, lbr_sem,
    cs_sem, cr_sem, p1s_sem, p1r_sem, p2s_sem, p2r_sem, hs_sem, hr_sem, os_sem, or_sem,
):
    pp = lax.axis_index("pp")
    tp = lax.axis_index("tp")
    core = lax.rem(pp, 2)
    chip = lax.rem(lax.div(pp, 2), CHIPS)
    half = lax.div(pp, 2 * CHIPS)
    yl = lax.div(tp, 4)
    x = lax.rem(tp, 4)

    yl_peer = (pp, (1 - yl) * 4 + x)
    x_up = (pp, yl * 4 + lax.rem(x + 1, 4))
    x_down = (pp, yl * 4 + lax.rem(x + 3, 4))
    core_peer = (pp + 1 - 2 * core, tp)
    half_peer = (lax.rem(pp + 2 * CHIPS, 4 * CHIPS), tp)

    def tp_peer(j):
        return (pp, lax.rem(tp + j, TP))

    def chip_index(j):
        return lax.rem(chip + j, CHIPS)

    def chip_peer(j):
        return ((half * CHIPS + chip_index(j)) * 2 + core, tp)

    copies = {}

    def load(name, src, dst):
        copies[name] = pltpu.make_async_copy(src, dst, in_sem.at[len(copies)])

    for l in (2, 1, 0):
        load(("k", l), k_hbm.at[l], k_v.at[l])
        load(("q", l), q_hbm.at[l], q_v.at[l])
        load(("g", l), g_hbm.at[l], g_v.at[l])
    load("h", h_hbm, h_v)
    load("dn", dn_hbm, dn_v)
    load("up", up_hbm, up_v)
    for l in (2, 1, 0):
        load(("w", l), w_hbm.at[l], w_v.at[l])
    load("top", top_hbm.at[:, core, chip], top_v)
    first = [(name, LAYERS - 1) for name in "kqg"]
    for name in first:
        copies[name].start()

    barrier = pltpu.get_barrier_semaphore()
    for j in range(1, TP):
        pl.semaphore_signal(barrier, inc=1, device_id=tp_peer(j), device_id_type=MESH)
    for j in range(1, CHIPS):
        pl.semaphore_signal(barrier, inc=1, device_id=chip_peer(j), device_id_type=MESH)
    for peer in (core_peer, half_peer):
        pl.semaphore_signal(barrier, inc=1, device_id=peer, device_id_type=MESH)

    def remote(src, dst, send, recv, device):
        return pltpu.make_async_remote_copy(
            src_ref=src, dst_ref=dst, send_sem=send, recv_sem=recv, device_id=device, device_id_type=MESH
        )

    def columns(row):
        return jnp.transpose(jnp.broadcast_to(row, (128, TOKENS)))

    def rows_of(sums):
        parts = [sums[128 * i : 128 * i + 128, :] for i in range(sums.shape[0] // 128)]
        return jnp.concatenate([jnp.sum(jnp.transpose(part), axis=0, keepdims=True) for part in parts], axis=0)

    def columns_of(rows):
        return jnp.concatenate(
            [jnp.transpose(jnp.broadcast_to(rows[i : i + 1, :], (128, 128))) for i in range(rows.shape[0])], axis=0
        )

    doc_row = doc_ref[...].astype(F32)
    doc_col = columns(doc_row)
    key_pos = lax.broadcasted_iota(jnp.int32, (128, 128), 0)
    query_pos = lax.broadcasted_iota(jnp.int32, (128, 128), 1)
    for b in range(4):
        low = max(0, b - 2)
        for kb in range(low, b + 1):
            allowed = doc_col[128 * kb : 128 * kb + 128, :] == doc_row[:, 128 * b : 128 * b + 128]
            if kb == b:
                allowed = allowed & (key_pos <= query_pos)
            at = MASK_OFFSET[b] + 128 * (kb - low)
            mask_v[at : at + 128, :] = jnp.where(allowed, 0.0, -jnp.inf)
    loss_row = loss_ref[...].astype(F32)
    labels = lax.broadcasted_iota(jnp.int32, (SEGS, TOKENS), 0).astype(F32)
    member = jnp.where(labels == doc_row, 1.0, 0.0)
    counts = jnp.sum(member * loss_row, axis=1, keepdims=True)
    per_token = jnp.sum(member * (1.0 / jnp.maximum(counts, 1.0)), axis=0, keepdims=True)
    weights = columns(adv_ref[...].astype(F32) * loss_row * per_token * (TOKENS / SEGS))
    weight_v[...] = weights.reshape(2, 2, CHIPS, ROWS, 128)

    slot = x * 2 + yl
    other = x * 2 + (1 - yl)
    left = lax.rem(x + 3, 4) * 2
    right = lax.rem(x + 1, 4) * 2
    across = lax.rem(x + 2, 4) * 2

    def attention(l):
        for name in ("k", "q", "g"):
            copies[(name, l)].wait()
        if l == LAYERS - 1:
            for name in copies:
                if name not in first:
                    copies[name].start()
        for b in range(4):
            low, high = max(0, b - 2) * 128, (b + 1) * 128
            keys = k_v[l, low:high, :]
            mask = mask_v[MASK_OFFSET[b] : MASK_OFFSET[b] + high - low, :]
            mask4 = jnp.concatenate([mask] * 4, axis=1)
            total = None
            for part in range(2):
                heads = range(4 * part, 4 * part + 4)
                block = slice(128 * b, 128 * b + 128)
                queries = jnp.concatenate([q_v[l, block, HEAD * i : HEAD * i + HEAD] for i in heads], axis=0)
                grads = jnp.concatenate([g_v[l, block, HEAD * i : HEAD * i + HEAD] for i in heads], axis=0)
                scores = dot(keys, queries, ((1,), (1,))) + mask4
                peak = jnp.max(scores, axis=0, keepdims=True)
                expo = jnp.exp2((scores - peak) * SOFTMAX_SCALE)
                probs = (expo * (1.0 / jnp.sum(expo, axis=0, keepdims=True))).astype(BF16)
                piece = dot(probs, grads, ((1,), (0,)))
                total = piece if total is None else total + piece
            if b == 0:
                acc_v[0:128, :] = total
            else:
                acc_v[low : high - 128, :] += total[: high - low - 128]
                acc_v[high - 128 : high, :] = total[high - low - 128 :]
        vg_v[l, slot] = acc_v[...].astype(BF16)

    def spans(chunk):
        return pl.ds(chunk[1], chunk[2])

    def tokens(chunk):
        return slice(chunk[1] * SPAN, (chunk[1] + chunk[2]) * SPAN)

    def index(chunk):
        return chunk[0] * 2 + chunk[1]

    def gather_copy(chunk, i, place, device):
        part = vg_v.at[chunk[0], place, pl.ds(chunk[1] * SPAN, chunk[2] * SPAN)]
        return remote(part, part, gs_sem.at[index(chunk), i], gr_sem.at[index(chunk), i], device)

    def gather_out(chunk, i):
        return (
            lambda: gather_copy(chunk, 0, slot, yl_peer),
            lambda: gather_copy(chunk, 1, slot, x_up),
            lambda: gather_copy(chunk, 2, slot, x_down),
            lambda: gather_copy(chunk, 3, other, x_up),
            lambda: gather_copy(chunk, 4, other, x_down),
            lambda: gather_copy(chunk, 5, left + yl, x_up),
            lambda: gather_copy(chunk, 6, right + (1 - yl), x_down),
        )[i]()

    def gather_in(chunk, i):
        place = (other, left + yl, right + yl, left + (1 - yl), right + (1 - yl), across + yl, across + (1 - yl))[i]
        return gather_copy(chunk, i, place, yl_peer)

    def gather_1(chunk):
        for i in (0, 1, 2):
            gather_out(chunk, i).start()

    def gather_2(chunk):
        gather_in(chunk, 0).wait_recv()
        for i in (3, 4):
            gather_out(chunk, i).start()

    def gather_3(chunk):
        gather_in(chunk, 1).wait_recv()
        gather_out(chunk, 5).start()

    def gather_4(chunk):
        gather_in(chunk, 4).wait_recv()
        gather_out(chunk, 6).start()

    def gather_end(chunk):
        for i in (2, 3, 5, 6):
            gather_in(chunk, i).wait_recv()

    def along_copy(chunk, i, place, device, first=0, count=SPAN):
        part = vg_v.at[chunk[0], place, pl.ds(chunk[1] * SPAN + first, count)]
        return remote(part, part, gs_sem.at[index(chunk), i], gr_sem.at[index(chunk), i], device)

    def along_out(chunk, i):
        return (
            lambda: along_copy(chunk, 0, slot, yl_peer),
            lambda: along_copy(chunk, 1, slot, x_up),
            lambda: along_copy(chunk, 2, slot, x_down),
            lambda: along_copy(chunk, 3, left + yl, yl_peer),
            lambda: along_copy(chunk, 4, right + yl, yl_peer),
            lambda: along_copy(chunk, 5, left + yl, x_up, 0, HALF),
            lambda: along_copy(chunk, 6, right + yl, x_down, HALF, HALF),
            lambda: along_copy(chunk, 7, across + yl, yl_peer),
        )[i]()

    def along_in(chunk, i):
        return (
            lambda: along_copy(chunk, 0, other, yl_peer),
            lambda: along_copy(chunk, 1, left + yl, x_up),
            lambda: along_copy(chunk, 2, right + yl, x_down),
            lambda: along_copy(chunk, 3, left + (1 - yl), yl_peer),
            lambda: along_copy(chunk, 4, right + (1 - yl), yl_peer),
            lambda: along_copy(chunk, 5, across + yl, x_up, 0, HALF),
            lambda: along_copy(chunk, 6, across + yl, x_down, HALF, HALF),
            lambda: along_copy(chunk, 7, across + (1 - yl), yl_peer),
        )[i]()

    def along_1(chunk):
        for i in (1, 2, 0):
            along_out(chunk, i).start()

    def along_2(chunk):
        along_in(chunk, 1).wait_recv()
        along_in(chunk, 2).wait_recv()
        for i in (5, 6, 3, 4):
            along_out(chunk, i).start()

    def along_3(chunk):
        along_in(chunk, 5).wait_recv()
        along_in(chunk, 6).wait_recv()
        along_out(chunk, 7).start()

    def along_end(chunk):
        for i in (0, 3, 4, 7):
            along_in(chunk, i).wait_recv()

    def squares_and_low():
        sqs_v[...] = jnp.zeros((16, 128), F32)
        copies["h"].wait()
        copies["dn"].wait()
        for l in range(LAYERS):
            sums = None
            for n in range(WIDTH // 128):
                part = h_v[l, :, 128 * n : 128 * n + 128].astype(F32)
                sums = part * part if sums is None else sums + part * part
            sqs_v[4 * l : 4 * l + 4, :] = rows_of(sums)
            hd_v[l] = dot(h_v[l], dn_v[l], ((1,), (1,)))
        sqr_v[tp] = sqs_v[...]

    def squares_copy(j, place):
        return remote(sqs_v, sqr_v.at[place], sqs_sem.at[j - 1], sqr_sem.at[j - 1], tp_peer(j))

    def squares_send():
        for j in range(1, TP):
            squares_copy(j, tp).start()

    def squares_wait():
        for j in range(1, TP):
            squares_copy(j, lax.rem(tp - j + TP, TP)).wait_recv()
        total = sqr_v[0]
        for i in range(1, TP):
            total = total + sqr_v[i]
        inverse = lax.rsqrt(total * (1.0 / MODEL) + 1e-5)
        for l in range(LAYERS):
            inv_v[l] = columns_of(inverse[4 * l : 4 * l + 4, :])

    def gathered(l, rows):
        return jnp.concatenate([vg_v[l, (j % 4) * 2 + j // 4, rows] for j in range(TP)], axis=1)

    def inner_copy(chunk, j, place):
        at = index(chunk)
        return remote(ins_v.at[at], inr_v.at[at, place], ins_sem.at[at, j - 1], inr_sem.at[at, j - 1], tp_peer(j))

    def products(chunk):
        l, at, rows = chunk[0], index(chunk), tokens(chunk)
        if l == LAYERS - 1 and chunk[1] == 0:
            copies["up"].wait()
        if chunk[1] == 0:
            copies[("w", l)].wait()
        ad_v[l, rows] = dot(gathered(l, rows), up_v[l], ((1,), (1,))).astype(BF16)
        acc_v[rows] = jnp.zeros((chunk[2] * SPAN, 128), F32)

        def one(n, unused):
            cols = pl.ds(pl.multiple_of(n * 512, 512), 512)
            twice = (ad_v[l, rows].astype(F32) * 2.0).astype(BF16)
            ng = dot(gathered(l, rows), w_v[l, cols, :], ((1,), (1,))) + dot(twice, dn_v[l, :, cols], ((1,), (0,)))
            ng_v[l % 2, rows, cols] = ng
            prod = h_v[l, rows, cols].astype(F32) * ng
            acc_v[rows] += (prod[:, :128] + prod[:, 128:256]) + (prod[:, 256:384] + prod[:, 384:])
            return unused

        lax.fori_loop(0, WIDTH // 512, one, 0)
        row = rows_of(acc_v[rows])
        ins_v[at] = jnp.concatenate([row] * (4 // chunk[2]), axis=0)
        inr_v[at, tp] = ins_v[at]
        for j in range(1, TP):
            inner_copy(chunk, j, tp).start()

    def terms(chunk):
        l, at, rows = chunk[0], index(chunk), tokens(chunk)
        for j in range(1, TP):
            inner_copy(chunk, j, lax.rem(tp - j + TP, TP)).wait_recv()
        total = inr_v[at, 0]
        for i in range(1, TP):
            total = total + inr_v[at, i]
        inv = inv_v[l, rows]
        acc_v[rows] = inv * inv * inv * columns_of(total[0 : 2 * chunk[2], :]) * (1.0 / MODEL)

        def one(n, unused):
            cols = pl.ds(pl.multiple_of(n * 128, 128), 128)
            term = inv_v[l, rows] * ng_v[l % 2, rows, cols] - acc_v[rows] * h_v[l, rows, cols].astype(F32)
            t_v[l, spans(chunk), :, :, cols] = term.astype(BF16).reshape(chunk[2], 2, HALF, 128)
            return unused

        lax.fori_loop(0, WIDTH // 128, one, 0)

    def lora_b_copy(l, j, block, place):
        return remote(lbs_v.at[l, block], lbr_v.at[l, place], lbs_sem.at[l, j - 1], lbr_sem.at[l, j - 1], tp_peer(j))

    def adapters(l):
        inv = inv_v[l][:, :RANK]
        scaled = (2.0 * inv * ad_v[l].astype(F32)).astype(BF16)
        la_v[l] = dot(scaled, h_v[l], ((0,), (0,)))
        low = (2.0 * inv * hd_v[l]).astype(BF16)
        part = dot(low, gathered(l, slice(0, TOKENS)), ((0,), (0,)))
        for j in range(TP):
            lbs_v[l, j] = part[:, 128 * j : 128 * j + 128].astype(BF16)
        lbr_v[l, tp] = lbs_v[l, tp]
        for j in range(1, TP):
            lora_b_copy(l, j, lax.rem(tp + j, TP), tp).start()
        pltpu.make_async_copy(la_v.at[l], la_hbm.at[l], out_sem.at[l]).start()

    def adapters_end(l):
        for j in range(1, TP):
            lora_b_copy(l, j, 0, lax.rem(tp - j + TP, TP)).wait_recv()
        total = lbr_v[l, 0].astype(F32)
        for i in range(1, TP):
            total = total + lbr_v[l, i].astype(F32)
        lb_v[l] = total
        pltpu.make_async_copy(lb_v.at[l], lb_hbm.at[l], out_sem.at[LAYERS + l]).start()

    def core_copy(chunk):
        at = index(chunk)
        return remote(
            t_v.at[chunk[0], spans(chunk), 1 - core], tp_v.at[chunk[0], spans(chunk)],
            cs_sem.at[at], cr_sem.at[at], core_peer,
        )

    def to_owner(chunk, j, place):
        at = index(chunk)
        return remote(
            p_v.at[chunk[0], spans(chunk), chip_index(j)], q8_v.at[chunk[0], place, spans(chunk)],
            p1s_sem.at[at, j - 1], p1r_sem.at[at, j - 1], chip_peer(j),
        )

    def from_owner(chunk, j, place):
        at = index(chunk)
        return remote(
            rs_v.at[chunk[0], chip_index(j), spans(chunk)], rr_v.at[chunk[0], spans(chunk), place],
            p2s_sem.at[at, j - 1], p2r_sem.at[at, j - 1], chip_peer(j),
        )

    def source(j):
        return lax.rem(chip - j + CHIPS, CHIPS)

    def pair_sums(chunk):
        l, ts = chunk[0], spans(chunk)
        core_copy(chunk).wait_recv()
        both = t_v[l, ts, core].astype(F32) + tp_v[l, ts].astype(F32)
        p_v[l, ts] = both.reshape(chunk[2], CHIPS, ROWS, WIDTH).astype(BF16)
        for j in (2, 1, 3):
            to_owner(chunk, j, chip).start()
        q8_v[l, chip, ts] = p_v[l, ts, chip]

    def total_copy(chunk):
        at = index(chunk)
        return remote(
            tots_v.at[chunk[0], spans(chunk)], totr_v.at[chunk[0], spans(chunk)],
            hs_sem.at[at], hr_sem.at[at], half_peer,
        )

    def totals(chunk):
        l, ts = chunk[0], spans(chunk)
        for j in range(1, CHIPS):
            to_owner(chunk, j, source(j)).wait_recv()
        total = q8_v[l, 0, ts].astype(F32)
        for i in range(1, CHIPS):
            total = total + q8_v[l, i, ts].astype(F32)
        tots_v[l, ts] = total.astype(BF16)
        total_copy(chunk).start()

    def suffix(chunk):
        l, ts = chunk[0], spans(chunk)
        if l == LAYERS - 1:
            if chunk[1] == 0:
                copies["top"].wait()
            weights = jnp.concatenate([weight_v[ts, core, chip]] * (WIDTH // 128), axis=2)
            carry = weights * top_v[ts].astype(F32)
        else:
            carry = carry_v[ts]
        total_copy(chunk).wait_recv()
        above = totr_v[l, ts].astype(F32)
        carry_v[ts] = carry + above + tots_v[l, ts].astype(F32)
        carry = carry + (1 - half).astype(F32) * above
        for i in reversed(range(CHIPS)):
            rs_v[l, i, ts] = carry.astype(BF16)
            carry = carry + q8_v[l, i, ts].astype(F32)
        for j in (2, 1, 3):
            from_owner(chunk, j, chip).start()
        rr_v[l, ts, chip] = rs_v[l, chip, ts]

    def out_copy(chunk):
        at = index(chunk)
        return remote(
            peer_v.at[chunk[0], spans(chunk)], out_hbm.at[chunk[0], spans(chunk), core],
            os_sem.at[at], or_sem.at[at], core_peer,
        )

    def out_in(chunk):
        at = index(chunk)
        return remote(
            peer_v.at[chunk[0], spans(chunk)], out_hbm.at[chunk[0], spans(chunk), 1 - core],
            os_sem.at[at], or_sem.at[at], core_peer,
        )

    def out_here(chunk):
        return pltpu.make_async_copy(
            own_v.at[chunk[0], spans(chunk)], out_hbm.at[chunk[0], spans(chunk), core], out_sem.at[2 * LAYERS + index(chunk)]
        )

    def finish(chunk):
        l, ts = chunk[0], spans(chunk)
        for j in range(1, CHIPS):
            from_owner(chunk, j, source(j)).wait_recv()
        first = (1 - core).astype(F32)
        second = core.astype(F32)
        carry = rr_v[l, ts].astype(F32).reshape(chunk[2], HALF, WIDTH)
        term = t_v[l, ts, core].astype(F32)
        peer_term = tp_v[l, ts].astype(F32)
        peer_v[l, ts] = (carry + peer_term + second * term).astype(BF16)
        out_copy(chunk).start()
        own_v[l, ts] = (carry + term + first * peer_term).astype(BF16)
        out_here(chunk).start()

    attention(2)
    pl.semaphore_wait(barrier, TP + CHIPS)
    along_1((2, 0, 1))
    gather_1((2, 1, 1))
    attention(1)
    gather_1((1, 0, 1))
    along_1((1, 1, 1))
    squares_and_low()
    squares_send()
    along_2((2, 0, 1))
    gather_2((2, 1, 1))
    gather_2((1, 0, 1))
    along_3((2, 0, 1))
    along_2((1, 1, 1))
    attention(0)
    gather_3((2, 1, 1))
    gather_4((2, 1, 1))
    squares_wait()
    gather_4((1, 0, 1))
    along_3((1, 1, 1))
    gather_3((1, 0, 1))
    along_end((2, 0, 1))
    products((2, 0, 1))
    gather_1((0, 0, 1))
    along_1((0, 1, 1))
    gather_end((2, 1, 1))
    products((2, 1, 1))
    gather_end((1, 0, 1))
    products((1, 0, 1))
    gather_2((0, 0, 1))
    gather_3((0, 0, 1))
    along_end((1, 1, 1))
    terms((2, 0, 1))
    core_copy((2, 0, 1)).start()
    products((1, 1, 1))
    pair_sums((2, 0, 1))
    terms((2, 1, 1))
    core_copy((2, 1, 1)).start()
    along_2((0, 1, 1))
    gather_4((0, 0, 1))
    terms((1, 0, 1))
    core_copy((1, 0, 1)).start()
    pair_sums((2, 1, 1))
    adapters(2)
    pair_sums((1, 0, 1))
    along_3((0, 1, 1))
    terms((1, 1, 1))
    core_copy((1, 1, 1)).start()
    gather_end((0, 0, 1))
    totals((2, 0, 1))
    products((0, 0, 1))
    pair_sums((1, 1, 1))
    totals((2, 1, 1))
    along_end((0, 1, 1))
    products((0, 1, 1))
    suffix((2, 0, 1))
    terms((0, 0, 1))
    totals((1, 0, 1))
    suffix((2, 1, 1))
    core_copy((0, 0, 1)).start()
    totals((1, 1, 1))
    terms((0, 1, 1))
    pair_sums((0, 0, 1))
    core_copy((0, 1, 1)).start()
    pair_sums((0, 1, 1))
    suffix((1, 0, 1))
    adapters_end(2)
    adapters(1)
    adapters(0)
    finish((2, 0, 1))
    totals((0, 0, 1))
    suffix((1, 1, 1))
    finish((2, 1, 1))
    totals((0, 1, 1))
    suffix((0, 0, 1))
    suffix((0, 1, 1))
    finish((1, 0, 1))
    finish((0, 0, 1))
    adapters_end(1)
    adapters_end(0)
    finish((1, 1, 1))
    finish((0, 1, 1))

    for chunk in GATHER_CHUNKS:
        for i in range(7):
            gather_out(chunk, i).wait_send()
    for chunk in ALONG_CHUNKS:
        for i in range(8):
            along_out(chunk, i).wait_send()
    for chunk in PRODUCT_CHUNKS:
        for j in range(1, TP):
            inner_copy(chunk, j, tp).wait_send()
    for chunk in SUM_CHUNKS:
        out_in(chunk).wait_recv()
        out_copy(chunk).wait_send()
        out_here(chunk).wait()
        core_copy(chunk).wait_send()
        total_copy(chunk).wait_send()
        for j in range(1, CHIPS):
            to_owner(chunk, j, chip).wait_send()
            from_owner(chunk, j, chip).wait_send()
    for l in range(LAYERS):
        pltpu.make_async_copy(la_v.at[l], la_hbm.at[l], out_sem.at[l]).wait()
        pltpu.make_async_copy(lb_v.at[l], lb_hbm.at[l], out_sem.at[LAYERS + l]).wait()
        for j in range(1, TP):
            lora_b_copy(l, j, lax.rem(tp + j, TP), tp).wait_send()
    for j in range(1, TP):
        squares_copy(j, tp).wait_send()


def place(grad_ref, a_ref, b_ref, grad_out, a_out, b_out, grad_v, a_v, b_v, in_sem, out_sem):
    pieces = [(a_ref, a_v, a_out), (b_ref, b_v, b_out)]
    for l in range(LAYERS):
        for t in range(2):
            at = (l, t)
            pieces.append((grad_ref.at[at], grad_v.at[at], grad_out.at[at]))
    reads = [pltpu.make_async_copy(src, mid, in_sem.at[i]) for i, (src, mid, _) in enumerate(pieces)]
    writes = [pltpu.make_async_copy(mid, dst, out_sem.at[i]) for i, (_, mid, dst) in enumerate(pieces)]
    for copy in reads:
        copy.start()
    for read, write in zip(reads, writes):
        read.wait()
        write.start()
    for copy in writes:
        copy.wait()


def per_device(
    queries, attention_output_grads, keys, hidden, value_weight, value_down_matrix, value_up_matrix,
    document_index, advantage, loss_token_mask, top_stream_gradient,
):
    hbm = pl.BlockSpec(memory_space=pl.ANY)
    vmem = pl.BlockSpec(memory_space=pltpu.VMEM)
    dma = pltpu.SemaphoreType.DMA
    scratch = [
        pltpu.VMEM((LAYERS, TOKENS, WIDTH), BF16),
        pltpu.VMEM((LAYERS, TOKENS, WIDTH), BF16),
        pltpu.VMEM((LAYERS, TOKENS, HEAD), BF16),
        pltpu.VMEM((LAYERS, TOKENS, WIDTH), BF16),
        pltpu.VMEM((LAYERS, WIDTH, WIDTH), BF16),
        pltpu.VMEM((LAYERS, RANK, WIDTH), BF16),
        pltpu.VMEM((LAYERS, RANK, WIDTH), BF16),
        pltpu.VMEM((2, ROWS, WIDTH), BF16),
        pltpu.VMEM((1152, 128), F32),
        pltpu.VMEM((2, 2, CHIPS, ROWS, 128), F32),
        pltpu.VMEM((TOKENS, 128), F32),
        pltpu.VMEM((LAYERS, TP, TOKENS, HEAD), BF16),
        pltpu.VMEM((LAYERS, TOKENS, RANK), F32),
        pltpu.VMEM((LAYERS, TOKENS, RANK), BF16),
        pltpu.VMEM((2, TOKENS, WIDTH), F32),
        pltpu.VMEM((LAYERS, TOKENS, 128), F32),
        pltpu.VMEM((16, 128), F32),
        pltpu.VMEM((TP, 16, 128), F32),
        pltpu.VMEM((2 * LAYERS, 8, 128), F32),
        pltpu.VMEM((2 * LAYERS, TP, 8, 128), F32),
        pltpu.VMEM((LAYERS, TP, RANK, HEAD), BF16),
        pltpu.VMEM((LAYERS, TP, RANK, HEAD), BF16),
        pltpu.VMEM((LAYERS, RANK, WIDTH), F32),
        pltpu.VMEM((LAYERS, RANK, HEAD), F32),
        pltpu.VMEM((LAYERS, 2, 2, HALF, WIDTH), BF16),
        pltpu.VMEM((LAYERS, 2, HALF, WIDTH), BF16),
        pltpu.VMEM((LAYERS, 2, CHIPS, ROWS, WIDTH), BF16),
        pltpu.VMEM((LAYERS, CHIPS, 2, ROWS, WIDTH), BF16),
        pltpu.VMEM((LAYERS, CHIPS, 2, ROWS, WIDTH), BF16),
        pltpu.VMEM((LAYERS, 2, CHIPS, ROWS, WIDTH), BF16),
        pltpu.VMEM((2, ROWS, WIDTH), F32),
        pltpu.VMEM((LAYERS, 2, ROWS, WIDTH), BF16),
        pltpu.VMEM((LAYERS, 2, ROWS, WIDTH), BF16),
        pltpu.VMEM((LAYERS, 2, HALF, WIDTH), BF16),
        pltpu.VMEM((LAYERS, 2, HALF, WIDTH), BF16),
        dma((16,)), dma((4 * LAYERS,)),
        dma((2 * LAYERS, 8)), dma((2 * LAYERS, 8)), dma((7,)), dma((7,)), dma((2 * LAYERS, 7)), dma((2 * LAYERS, 7)),
        dma((LAYERS, 7)), dma((LAYERS, 7)),
        dma((2 * LAYERS,)), dma((2 * LAYERS,)),
        dma((2 * LAYERS, 7)), dma((2 * LAYERS, 7)), dma((2 * LAYERS, 7)), dma((2 * LAYERS, 7)),
        dma((2 * LAYERS,)), dma((2 * LAYERS,)),
        dma((2 * LAYERS,)), dma((2 * LAYERS,)),
    ]
    grad_in, lora_a, lora_b = pl.pallas_call(
        kernel,
        name="value_backward",
        out_shape=(
            jax.ShapeDtypeStruct((LAYERS, 2, 2, HALF, WIDTH), BF16),
            jax.ShapeDtypeStruct((LAYERS, RANK, WIDTH), F32),
            jax.ShapeDtypeStruct((LAYERS, RANK, HEAD), F32),
        ),
        in_specs=[hbm] * 8 + [vmem] * 3,
        out_specs=(hbm, hbm, hbm),
        scratch_shapes=scratch,
        compiler_params=pltpu.CompilerParams(
            collective_id=0, has_side_effects=True, vmem_limit_bytes=60 << 20
        ),
        cost_estimate=pl.CostEstimate(flops=8_000_000_000, bytes_accessed=22_000_000, transcendentals=4_000_000),
    )(
        queries[0], attention_output_grads[0], keys[0], hidden[0], value_weight[0], jnp.swapaxes(value_down_matrix[0], 1, 2),
        value_up_matrix[0], top_stream_gradient.reshape(2, 2, CHIPS, ROWS, WIDTH),
        document_index.reshape(1, TOKENS), advantage.reshape(1, TOKENS), loss_token_mask.reshape(1, TOKENS),
    )
    grad_in, lora_a, lora_b = pl.pallas_call(
        place,
        name="place",
        out_shape=(
            jax.ShapeDtypeStruct(grad_in.shape, BF16),
            jax.ShapeDtypeStruct(lora_a.shape, F32),
            jax.ShapeDtypeStruct(lora_b.shape, F32),
        ),
        in_specs=[hbm] * 3,
        out_specs=(hbm, hbm, hbm),
        scratch_shapes=[
            pltpu.VMEM(grad_in.shape, BF16),
            pltpu.VMEM(lora_a.shape, F32),
            pltpu.VMEM(lora_b.shape, F32),
            dma((8,)), dma((8,)),
        ],
        compiler_params=pltpu.CompilerParams(vmem_limit_bytes=60 << 20),
    )(grad_in, lora_a, lora_b)
    return grad_in.reshape(1, LAYERS, TOKENS, WIDTH), jnp.swapaxes(lora_a, 1, 2)[None], lora_b[None]


def solution(mesh):
    in_specs = (
        P("pp", None, None, "tp"),
        P("pp", None, None, "tp"),
        P("pp", None, None, "tp"),
        P("pp", None, None, "tp"),
        P("pp", None, "tp", None),
        P("pp", None, "tp", None),
        P("pp", None, None, None),
        P(),
        P(),
        P(),
        P(None, "tp"),
    )
    out_specs = (P("pp", None, None, "tp"), P("pp", None, "tp", None), P("pp", None, None, "tp"))
    return jax.shard_map(
        per_device, mesh=mesh, in_specs=in_specs, out_specs=out_specs, check_vma=False
    )
```
